32 devices in a mesh: groups: 1, dp: 16 (over z, y, x), tensor: 2 (over core).
Axes of the slice: x: 2, y: 2, z: 4, core: 2. Of those that a mesh axis runs over, the one named last changes fastest.
Arguments:
- normed: bfloat16 [8192, 5120], P(('groups', 'dp')), may hold values from -6 to 6
- cotangent: bfloat16 [8192, 1024], P(('groups', 'dp'), 'tensor'), may hold values from -6 to 6
- value_weight: bfloat16 [5120, 1024], P('dp', 'tensor'), may hold values from -0.078125 to 0.078125
- adapter_down_maps: bfloat16 [5120, 512], P('dp', 'groups'), may hold values from -0.078125 to 0.078125
- adapter_up_maps: bfloat16 [8, 64, 1024], P('groups', None, 'tensor'), may hold values from -0.19921875 to 0.19921875
- tenant_devices: int32 [8], P('groups'), may hold values from 1 to 9, as said below
- adapter_of: int32 [8], P('groups'), may hold values from 0 to 7, each once
- valid_tokens: int32 [8], P('groups'), may hold values from 1 to 4608, as said below
Outputs:
- values: bfloat16 [8192, 1024], P(('groups', 'dp'), 'tensor')
- normed_input_gradient: bfloat16 [8192, 5120], P(('groups', 'dp'), 'tensor')
- grad_a: float32 [16, 64, 5120], P(('groups', 'dp'), None, 'tensor')
- grad_b: float32 [16, 64, 1024], P(('groups', 'dp'), None, 'tensor')
The draws below stay inside these ranges and needn't reach their ends.
Inputs may be any that keep to these rules, and one draw needn't show every extreme that they name: Slot s owns the next tenant_devices[s] shards along dp; the counts sum to 16, and the largest is exactly 9. valid_tokens[s] exceeds 512 times (tenant_devices[s] - 1) and is at most 512 times tenant_devices[s]; it equals that bound for the slot with the most devices. `adapter_of`: each adapter serves exactly one slot.
All inputs are finite; a program needn't handle non-finite values.
Results may differ from the reference program's by a relative error of at most 0.0032.
Values may be sent and summed in bfloat16 or wider, within the bound.
No kernel may reach another device: no remote copies, remote signals or barrier semaphores. Data moves between devices by JAX's collectives and lax.ppermute only.
A program may use at most 128 MiB of HBM per device.

```python
import jax
import jax.numpy as jnp

MODEL_DIM = 5120
VALUE_WIDTH = 1024
ADAPTER_RANK = 64
TENANT_TOTAL = 8
TOK_DEV = 512
TOKEN_ROWS = 8192
MOST = 9
N_DP = 16


def tenant_layout(key):
    slot_ids = jnp.arange(TENANT_TOTAL, dtype=jnp.int32)
    busiest = jax.random.randint(jax.random.fold_in(key, 11), (), 0, TENANT_TOTAL)
    weights = jax.random.randint(jax.random.fold_in(key, 12), (TENANT_TOTAL,), 1, 9)
    is_busiest = slot_ids == busiest
    weights = jnp.where(is_busiest, 0, weights)
    extra_total = N_DP - MOST - (TENANT_TOTAL - 1)
    extra_units = extra_total * weights // jnp.sum(weights)
    leftover = extra_total - jnp.sum(extra_units)
    others_rank = jnp.cumsum(jnp.where(is_busiest, 0, 1)) - 1
    bump_units = jnp.where(jnp.logical_and(jnp.logical_not(is_busiest), others_rank < leftover), 1, 0)
    counts = jnp.where(is_busiest, MOST, 1 + extra_units + bump_units).astype(jnp.int32)
    pad_rows = jax.random.randint(jax.random.fold_in(key, 13), (TENANT_TOTAL,), 0, TOK_DEV)
    pad_rows = jnp.where(is_busiest, 0, pad_rows).astype(jnp.int32)
    return (counts, pad_rows)


def draw_tenant_devices(key, part):
    counts, pad_rows = tenant_layout(key)
    return counts


def draw_valid_tokens(key, part):
    counts, pad_rows = tenant_layout(key)
    return (counts * TOK_DEV - pad_rows).astype(jnp.int32)


def block_levels(rng, dims, shards, low, high):
    def one(dim, shards_of):
        steps = jax.random.uniform(jax.random.fold_in(jax.random.fold_in(rng, 6), dim), (shards_of,), jnp.float32, low / len(shards), high / len(shards))
        return jnp.repeat(jnp.exp(steps), dims[dim] // shards_of).reshape((-1,) + (1,) * (len(dims) - dim - 1))

    factor_of = one(*shards[0])
    for cut in shards[1:]:
        factor_of = factor_of * one(*cut)
    return factor_of


def bell_draw(stream_key, dims, spread, reach, pieces=(), kind=jnp.bfloat16):
    result = spread * jax.random.normal(stream_key, dims, jnp.float32)
    if pieces:
        result = result * block_levels(stream_key, dims, pieces, -0.22, 0.18)
    return jnp.clip(result, -reach, reach).astype(kind)


def setup_inputs(seed: int = 0, part: int = 0) -> dict:
    splits = jax.random.split(jax.random.key(seed), 9)
    own_keys = jax.random.split(jax.random.fold_in(splits[8], part), 9)
    normed = bell_draw(own_keys[0], (TOKEN_ROWS, MODEL_DIM), 1.0, 6.0, ((0, 16),))
    cotangent = bell_draw(own_keys[1], (TOKEN_ROWS, VALUE_WIDTH), 1.0, 6.0, ((0, 16), (1, 2)))
    value_weight = bell_draw(splits[2], (MODEL_DIM, VALUE_WIDTH), MODEL_DIM ** -0.5, 0.078125, ((0, 16), (1, 2)))
    adapter_down_maps = bell_draw(own_keys[3], (MODEL_DIM, TENANT_TOTAL * ADAPTER_RANK), MODEL_DIM ** -0.5, 0.078125, ((0, 16),))
    adapter_up_maps = bell_draw(own_keys[4], (TENANT_TOTAL, ADAPTER_RANK, VALUE_WIDTH), 0.03, 0.19921875, ((2, 2),))
    tenant_devices = draw_tenant_devices(jax.random.fold_in(jax.random.fold_in(splits[8], part), 71), part)
    adapter_of = jax.random.permutation(own_keys[6], TENANT_TOTAL).astype(jnp.int32)
    valid_tokens = draw_valid_tokens(jax.random.fold_in(jax.random.fold_in(splits[8], part), 71), part)
    return {"normed": normed, "cotangent": cotangent, "value_weight": value_weight, "adapter_down_maps": adapter_down_maps, "adapter_up_maps": adapter_up_maps, "tenant_devices": tenant_devices, "adapter_of": adapter_of, "valid_tokens": valid_tokens}


def reference(normed, cotangent, value_weight, adapter_down_maps, adapter_up_maps, tenant_devices, adapter_of, valid_tokens):
    slot_ends = jnp.cumsum(tenant_devices).astype(jnp.int32)
    device_ids = jnp.arange(N_DP, dtype=jnp.int32)
    tenant_slot = jnp.sum((slot_ends[None, :] <= device_ids[:, None]).astype(jnp.int32), axis=1)
    first_device = (slot_ends - tenant_devices)[tenant_slot]
    adapter_index = adapter_of[tenant_slot]
    valid_count = valid_tokens[tenant_slot]
    row_ids = jnp.arange(TOK_DEV, dtype=jnp.int32)
    position = (device_ids - first_device)[:, None] * TOK_DEV + row_ids[None, :]
    keep_rows = (position < valid_count[:, None]).reshape(TOKEN_ROWS)
    adapter_down_weight = jnp.transpose(adapter_down_maps.reshape(MODEL_DIM, TENANT_TOTAL, ADAPTER_RANK)[:, adapter_index, :], (1, 0, 2)).astype(jnp.float32)
    adapter_up_weight = adapter_up_maps[adapter_index].astype(jnp.float32)
    normed_input_block = normed.reshape(N_DP, TOK_DEV, MODEL_DIM).astype(jnp.float32)
    rank_projection = jnp.einsum('hlo,hos->hls', normed_input_block, adapter_down_weight).astype(jnp.bfloat16)
    frozen_output = jnp.dot(normed, value_weight, preferred_element_type=jnp.float32)
    adapter_output = jnp.einsum('ads,asv->adv', rank_projection.astype(jnp.float32), adapter_up_weight).reshape(TOKEN_ROWS, VALUE_WIDTH)
    values = (frozen_output + 2.0 * adapter_output).astype(jnp.bfloat16)
    masked = jnp.where(keep_rows[:, None], cotangent, jnp.zeros_like(cotangent))
    tenant_masked_block = masked.reshape(N_DP, TOK_DEV, VALUE_WIDTH).astype(jnp.float32)
    backward_rank_term = jnp.einsum('foj,fcj->foc', tenant_masked_block, adapter_up_weight)
    scaled = (2.0 * backward_rank_term).astype(jnp.bfloat16)
    scaled_value_rows = scaled.astype(jnp.float32)
    frozen_gradient = jnp.dot(masked, value_weight.T, preferred_element_type=jnp.float32)
    adapter_gradient = jnp.einsum('blf,bjf->blj', scaled_value_rows, adapter_down_weight).reshape(TOKEN_ROWS, MODEL_DIM)
    normed_input_gradient = (frozen_gradient + adapter_gradient).astype(jnp.bfloat16)
    term_a = jnp.einsum('ntr,ntd->nrd', scaled_value_rows, normed_input_block)
    term_b = 2.0 * jnp.einsum('ntr,ntk->nrk', rank_projection.astype(jnp.float32), tenant_masked_block)
    slot_sums_a = jax.ops.segment_sum(term_a, tenant_slot, num_segments=TENANT_TOTAL)
    slot_sums_b = jax.ops.segment_sum(term_b, tenant_slot, num_segments=TENANT_TOTAL)
    grad_a = slot_sums_a[tenant_slot]
    grad_b = slot_sums_b[tenant_slot]
    return values, normed_input_gradient, grad_a, grad_b
```

```python
import functools

import jax
import jax.numpy as jnp
from jax import lax
from jax.experimental import pallas as pl
from jax.experimental.pallas import tpu as pltpu
from jax.sharding import PartitionSpec as P

CHUNKS = (1, 1)


def dot(left, right, left_dim, right_dim):
    return lax.dot_general(
        left,
        right,
        (((left_dim,), (right_dim,)), ((), ())),
        preferred_element_type=jnp.float32,
    )


def swap_cores(x):
    n = lax.axis_size("tensor")
    return lax.ppermute(x, "tensor", [(i, n - 1 - i) for i in range(n)])


def exchange(x, mask):
    return lax.ppermute(x, "dp", [(i, i ^ mask) for i in range(lax.axis_size("dp"))])


def pick(pieces, index):
    result = pieces[0]
    for i in range(1, len(pieces)):
        result = jnp.where(index == i, pieces[i], result)
    return result


def place_kernel(plan, count, *refs):
    sources, outs, sems = refs[:-3], refs[-3:-1], refs[-1]
    half = count // 2
    key = lax.axis_index("dp") ^ (lax.axis_index("tensor") * half)
    copies = []
    for number, (source, slot, mask, start, rows) in enumerate(plan):
        block = key ^ mask
        for part in range(2):
            copy = pltpu.make_async_copy(
                sources[source].at[slot],
                outs[part].at[block % half, pl.ds(start, rows)],
                sems.at[number],
            )
            copies.append((block // half == part, copy))
    for here, copy in copies:
        pl.when(here)(copy.start)
    for here, copy in copies:
        pl.when(here)(copy.wait)


def place(plan, sources, count, rows, columns):
    shape = jax.ShapeDtypeStruct((count // 2, rows, columns), sources[0].dtype)
    return pl.pallas_call(
        functools.partial(place_kernel, plan, count),
        out_shape=(shape, shape),
        in_specs=[pl.BlockSpec(memory_space=pl.ANY)] * len(sources),
        out_specs=[pl.BlockSpec(memory_space=pltpu.VMEM)] * 2,
        scratch_shapes=[pltpu.SemaphoreType.DMA((len(plan),))],
        compiler_params=pltpu.CompilerParams(vmem_limit_bytes=32 * 1024 * 1024),
        cost_estimate=pl.CostEstimate(
            flops=0, bytes_accessed=4 * count * rows * columns, transcendentals=0
        ),
    )(*sources)


def gather_rows(piece):
    count = lax.axis_size("dp")
    rows, columns = piece.shape
    low_masks = []
    mask = 1
    while mask < count // 4:
        low_masks.append(mask)
        mask *= 2
    high_masks = (0, count // 4, count // 2, 3 * count // 4)
    blocks = [piece] + [exchange(piece, m) for m in high_masks[1:]]
    stack = jnp.stack(blocks)
    plan, sources = [], []
    cut = (rows // 2 + 15) // 16 * 16
    for part, (begin, end) in enumerate(((0, cut), (cut, rows))):
        held = stack[:, begin:end]
        masks = list(high_masks)
        order = low_masks if part == 0 else low_masks[::-1]
        for step, m in enumerate(order):
            other = exchange(held, m)
            other_masks = [k ^ m for k in masks]
            if step < len(order) - 1:
                held = jnp.concatenate([held, other])
                masks = masks + other_masks
        for array, array_masks in ((held, masks), (other, other_masks)):
            for slot, k in enumerate(array_masks):
                plan.append((len(sources), slot, k, begin, end - begin))
            sources.append(array)
    mine, other = place(tuple(plan), sources, count, rows, columns)
    return mine.reshape(count // 2 * rows, columns), other.reshape(count // 2 * rows, columns)


def prepare_kernel(
    devices_ref, adapter_ref, valid_ref, down_ref, up_ref, cotangent_ref,
    masked_ref, back_ref, up_out_ref, blocks_ref, shared_ref, ids_ref,
):
    count = lax.axis_size("dp")
    position = lax.axis_index("dp")
    tenant_count = devices_ref.shape[0]
    row_count = cotangent_ref.shape[0]
    _, rank, width = up_ref.shape
    zero = jnp.int32(0)
    end, own_id, first, valid, devices = zero, zero, zero, zero, zero
    ids = [zero] * count
    for slot in range(tenant_count):
        start = end
        end = end + devices_ref[slot]
        adapter = adapter_ref[slot]
        mine = jnp.logical_and(start <= position, position < end)
        own_id = jnp.where(mine, adapter, own_id)
        first = jnp.where(mine, start, first)
        valid = jnp.where(mine, valid_ref[slot], valid)
        devices = jnp.where(mine, devices_ref[slot], devices)
        for i in range(count):
            ids[i] = jnp.where(jnp.logical_and(start <= i, i < end), adapter, ids[i])
    for i in range(count):
        ids_ref[i] = ids[i]
    shared_ref[0] = (devices > 1).astype(jnp.int32)
    rows = lax.broadcasted_iota(jnp.int32, (row_count, width), 0)
    keep = (position - first) * row_count + rows < valid
    masked = jnp.where(keep, cotangent_ref[...], jnp.zeros_like(cotangent_ref[...]))
    masked_ref[...] = masked
    up = up_ref[own_id]
    up_out_ref[...] = up
    back_ref[...] = dot(up, masked, 1, 1)
    low_count = count // 4
    quarter = down_ref.shape[0] // 4
    total = down_ref.shape[1]
    base = lax.axis_index("tensor") * (2 * quarter)
    upper = down_ref[pl.ds(pl.multiple_of(base, quarter), quarter), :]
    lower = down_ref[pl.ds(pl.multiple_of(base + quarter, quarter), quarter), :]
    source = lax.broadcasted_iota(jnp.int32, (total, 2 * rank), 0)
    lane = lax.broadcasted_iota(jnp.int32, (total, 2 * rank), 1)
    for m in range(count):
        target = ids_ref[position ^ m] * rank + lane
        pick_upper = (source == target).astype(jnp.float32)
        pick_upper = jnp.where(lane < rank, pick_upper, 0.0).astype(jnp.bfloat16)
        pick_lower = (source + rank == target).astype(jnp.float32)
        pick_lower = jnp.where(lane >= rank, pick_lower, 0.0).astype(jnp.bfloat16)
        block = dot(upper, pick_upper, 1, 0) + dot(lower, pick_lower, 1, 0)
        blocks_ref[m % low_count, m // low_count] = block.astype(jnp.bfloat16)


def prepare(devices, adapter_of, valid, down_maps, up_maps, cotangent, count):
    rows, total = down_maps.shape
    rank = up_maps.shape[1]
    smem = pl.BlockSpec(memory_space=pltpu.SMEM)
    vmem = pl.BlockSpec(memory_space=pltpu.VMEM)
    return pl.pallas_call(
        prepare_kernel,
        out_shape=(
            jax.ShapeDtypeStruct(cotangent.shape, cotangent.dtype),
            jax.ShapeDtypeStruct((rank, cotangent.shape[0]), jnp.float32),
            jax.ShapeDtypeStruct(up_maps.shape[1:], up_maps.dtype),
            jax.ShapeDtypeStruct((count // 4, 4, rows // 4, 2 * rank), down_maps.dtype),
            jax.ShapeDtypeStruct((1,), jnp.int32),
        ),
        in_specs=[smem] * 3 + [vmem] * 3,
        out_specs=[vmem] * 4 + [smem],
        scratch_shapes=[pltpu.SMEM((count,), jnp.int32)],
        compiler_params=pltpu.CompilerParams(vmem_limit_bytes=32 * 1024 * 1024),
    )(devices, adapter_of, valid, down_maps, up_maps, cotangent)


def low_kernel(rank, mine_refs, other_refs, normed_ref, low_ref, down_ref, full_ref):
    count = lax.axis_size("dp")
    position = lax.axis_index("dp")
    tensor_part = lax.axis_index("tensor")
    low_count = count // 4
    quarter = mine_refs[0].shape[-2]
    for refs, part in ((mine_refs, tensor_part), (other_refs, 1 - tensor_part)):
        for h, ref in enumerate(refs):
            for l in range(low_count):
                source = position ^ (h * low_count + l)
                block = ref[l]
                for side in range(2):
                    start = pl.multiple_of((source * 4 + part * 2 + side) * quarter, quarter)
                    full_ref[pl.ds(start, quarter), :] = block[:, side * rank : (side + 1) * rank]
    half = full_ref.shape[0] // 2
    low_ref[...] = dot(normed_ref[...], full_ref[...], 1, 0).astype(jnp.bfloat16)
    down_ref[...] = full_ref[pl.ds(pl.multiple_of(tensor_part * half, half), half), :]


def low_rank_of(mine, other, normed, rank):
    row_count, model_width = normed.shape

    def kernel(*refs):
        low_kernel(rank, refs[0:4], refs[4:8], *refs[8:])

    return pl.pallas_call(
        kernel,
        out_shape=(
            jax.ShapeDtypeStruct((row_count, rank), jnp.bfloat16),
            jax.ShapeDtypeStruct((model_width // 2, rank), jnp.bfloat16),
        ),
        in_specs=[pl.BlockSpec(memory_space=pltpu.VMEM)] * 9,
        out_specs=[pl.BlockSpec(memory_space=pltpu.VMEM)] * 2,
        scratch_shapes=[pltpu.VMEM((model_width, rank), jnp.bfloat16)],
        compiler_params=pltpu.CompilerParams(vmem_limit_bytes=40 * 1024 * 1024),
    )(*mine, *other, normed)


def send_blocks(blocks):
    low_count = blocks.shape[0]
    got = [blocks[0]] + [exchange(blocks[l], l) for l in range(1, low_count)]
    rows = [jnp.stack([g[h] for g in got]) for h in range(4)]
    return [rows[0]] + [exchange(rows[h], h * low_count) for h in range(1, 4)]


def sum_single_run(term, position):
    count = lax.axis_size("dp")
    low_count, high_step = count // 4, count // 4
    low, high = position % low_count, position // high_step
    rows, columns = term.shape
    part = rows // low_count

    def row_part(index):
        return lax.dynamic_slice_in_dim(term, index * part, part, 0)

    total = row_part(low)
    for m in range(1, low_count):
        total = total + exchange(row_part(low ^ m), m)
    width = columns // 4

    def column_part(index):
        return lax.dynamic_slice_in_dim(total, index * width, width, 1)

    share = column_part(high)
    for m in range(1, 4):
        share = share + exchange(column_part(high ^ m), m * high_step)
    share = share.astype(jnp.bfloat16)
    got = [share] + [exchange(share, m * high_step) for m in range(1, 4)]
    strip = jnp.concatenate([pick(got, high ^ i) for i in range(4)], axis=1)
    got = [strip] + [exchange(strip, m) for m in range(1, low_count)]
    return jnp.concatenate([pick(got, low ^ i) for i in range(low_count)], axis=0)


def shards(
    normed,
    cotangent,
    value_weight,
    adapter_down_maps,
    adapter_up_maps,
    tenant_devices,
    adapter_of,
    valid_tokens,
):
    row_count, model_width = normed.shape
    rank = adapter_up_maps.shape[1]
    tenant_count = tenant_devices.shape[0]
    width = value_weight.shape[1]
    count = lax.axis_size("dp")
    half_width = model_width // 2
    tensor_part = lax.axis_index("tensor")
    position = lax.axis_index("dp")

    if value_weight.shape[0] % 64 == 0:
        masked, back_half, up_matrix, blocks, shared = prepare(
            tenant_devices, adapter_of, valid_tokens, adapter_down_maps, adapter_up_maps, cotangent, count
        )
        shared = shared[0] > 0
        scaled_t = (2.0 * (back_half + swap_cores(back_half))).astype(jnp.bfloat16)
        mine = send_blocks(blocks)
        other = swap_cores(jnp.stack(mine))
        low_rank, down_keep = low_rank_of(mine, [other[h] for h in range(4)], normed, rank)
    else:
        slot_ends = jnp.cumsum(tenant_devices)
        tenant_slot = jnp.sum((slot_ends <= position).astype(jnp.int32))
        picker = (jnp.arange(tenant_count, dtype=jnp.int32) == tenant_slot).astype(jnp.int32)
        first_device = jnp.sum(picker * (slot_ends - tenant_devices))
        adapter_index = jnp.sum(picker * adapter_of)
        valid_count = jnp.sum(picker * valid_tokens)
        shared = jnp.sum(picker * tenant_devices) > 1
        offsets = (position - first_device) * row_count + jnp.arange(row_count, dtype=jnp.int32)
        keep_rows = offsets < valid_count
        up_matrix = lax.dynamic_index_in_dim(adapter_up_maps, adapter_index, 0, keepdims=False)
        masked = jnp.where(keep_rows[:, None], cotangent, jnp.zeros_like(cotangent))
        back_half = dot(up_matrix, masked, 1, 1)
        scaled_t = (2.0 * (back_half + swap_cores(back_half))).astype(jnp.bfloat16)
        down_maps = lax.all_gather(adapter_down_maps, "dp", axis=0, tiled=True)
        down_map = lax.dynamic_slice_in_dim(down_maps, adapter_index * rank, rank, 1)
        down_keep = lax.dynamic_slice_in_dim(down_map, tensor_part * half_width, half_width, 0)
        low_rank = dot(normed, down_map, 1, 0).astype(jnp.bfloat16)
    masked_other = swap_cores(masked)
    normed_keep = lax.dynamic_slice_in_dim(normed, tensor_part * half_width, half_width, 1)
    normed_give = lax.dynamic_slice_in_dim(normed, (1 - tensor_part) * half_width, half_width, 1)
    term_a = dot(scaled_t, normed_keep, 1, 0)
    term_b = 2.0 * dot(low_rank, masked, 0, 0)

    terms = jnp.concatenate([term_a, term_b], axis=1)
    most = 9 * count // 16
    if count - most == tenant_count - 1:
        total = sum_single_run(jnp.where(shared, terms, 0.0), position)
        grads = jnp.where(shared, total.astype(jnp.float32), terms)
    else:
        slot_ends = jnp.cumsum(tenant_devices)
        tenant_slot = jnp.sum((slot_ends <= position).astype(jnp.int32))
        marks = (jnp.arange(tenant_count, dtype=jnp.int32) == tenant_slot).astype(jnp.float32)
        totals = lax.psum(marks[:, None, None] * terms[None], "dp")
        grads = lax.dynamic_index_in_dim(totals, tenant_slot, 0, keepdims=False)
    grad_a, grad_b = grads[None, :, :half_width], grads[None, :, half_width:]

    gradient = dot(scaled_t, down_keep, 0, 1)
    values = []
    start = 0
    for share in CHUNKS:
        columns = width * share // sum(CHUNKS)
        stop = start + columns
        mine, give = gather_rows(value_weight[:, start:stop])
        other = swap_cores(give)
        base = dot(normed_keep, mine, 1, 0) + dot(normed_give, give, 1, 0)
        extra = dot(low_rank, up_matrix[:, start:stop], 1, 0)
        values.append((base + 2.0 * extra).astype(jnp.bfloat16))
        gradient = gradient + dot(masked[:, start:stop], mine, 1, 1)
        gradient = gradient + dot(masked_other[:, start:stop], other, 1, 1)
        start = stop
    values = jnp.concatenate(values, axis=1)
    return (values, gradient.astype(jnp.bfloat16), grad_a, grad_b)


def solution(mesh):
    return jax.shard_map(
        shards,
        mesh=mesh,
        in_specs=(
            P(("groups", "dp"), None),
            P(("groups", "dp"), "tensor"),
            P("dp", "tensor"),
            P("dp", "groups"),
            P("groups", None, "tensor"),
            P("groups"),
            P("groups"),
            P("groups"),
        ),
        out_specs=(
            P(("groups", "dp"), "tensor"),
            P(("groups", "dp"), "tensor"),
            P(("groups", "dp"), None, "tensor"),
            P(("groups", "dp"), None, "tensor"),
        ),
        check_vma=False,
    )
```

```python
import functools

import jax
import jax.numpy as jnp
from jax import lax
from jax.experimental import pallas as pl
from jax.experimental.pallas import tpu as pltpu
from jax.sharding import PartitionSpec as P

EXCHANGED = (1, 2)

HBM = pl.BlockSpec(memory_space=pltpu.HBM)
VMEM = pl.BlockSpec(memory_space=pltpu.VMEM)
SMEM = pl.BlockSpec(memory_space=pltpu.SMEM)


SHORT = pl.CostEstimate(flops=1, bytes_accessed=1, transcendentals=0)


def vmem_limit(mib):
    return pltpu.CompilerParams(vmem_limit_bytes=mib * 1024 * 1024)


def dot(left, right, left_dim, right_dim):
    return lax.dot_general(
        left,
        right,
        (((left_dim,), (right_dim,)), ((), ())),
        preferred_element_type=jnp.float32,
    )


def swap_cores(x):
    n = lax.axis_size("tensor")
    return lax.ppermute(x, "tensor", [(i, n - 1 - i) for i in range(n)])


def exchange(x, mask):
    return lax.ppermute(x, "dp", [(i, i ^ mask) for i in range(lax.axis_size("dp"))])


def pick(pieces, index):
    result = pieces[0]
    for i in range(1, len(pieces)):
        result = jnp.where(index == i, pieces[i], result)
    return result


def fence(x, *others):
    def kernel(*refs):
        pass

    return pl.pallas_call(
        kernel,
        out_shape=jax.ShapeDtypeStruct(x.shape, x.dtype),
        in_specs=[HBM] * (1 + len(others)),
        out_specs=HBM,
        input_output_aliases={0: 0},
        cost_estimate=SHORT,
    )(x, *others)


def kernel_call(body, ins, outs, scalars=(), raw=(), scratch=()):
    counts = (len(scalars), len(ins), len(raw), len(outs), len(ins), len(outs), len(scratch), 1)

    def kernel(*refs):
        groups, start = [], 0
        for count in counts:
            groups.append(refs[start : start + count])
            start += count
        scalar_refs, in_hbm, raw_refs, out_hbm, in_refs, out_refs, scratch_refs, (sems,) = groups
        loads = [
            pltpu.make_async_copy(source, target, sems.at[i])
            for i, (source, target) in enumerate(zip(in_hbm, in_refs))
        ]
        for load in loads:
            load.start()
        stores = []

        def get(i):
            loads[i].wait()
            return in_refs[i]

        def put(i):
            store = pltpu.make_async_copy(out_refs[i], out_hbm[i], sems.at[len(ins) + i])
            store.start()
            stores.append(store)

        body(scalar_refs, get, raw_refs, out_refs, put, scratch_refs)
        for store in stores:
            store.wait()

    return pl.pallas_call(
        kernel,
        out_shape=tuple(outs),
        in_specs=[SMEM] * len(scalars) + [HBM] * (len(ins) + len(raw)),
        out_specs=tuple([HBM] * len(outs)),
        scratch_shapes=[
            *[pltpu.VMEM(x.shape, x.dtype) for x in (*ins, *outs)],
            *scratch,
            pltpu.SemaphoreType.DMA((len(ins) + len(outs),)),
        ],
        compiler_params=vmem_limit(56),
        cost_estimate=SHORT,
    )(*scalars, *ins, *raw)


def high_masks():
    step = lax.axis_size("dp") // 4
    return (0, step, 2 * step, 3 * step)


def low_masks():
    masks, mask = [], 1
    while mask < lax.axis_size("dp") // 4:
        masks.append(mask)
        mask *= 2
    return masks


def first_phase(piece):
    low_count = lax.axis_size("dp") // 4
    slots = []
    for r in range(4):
        pairs = []
        for z in range(4):
            for t in range(2):
                source = 2 * t + (z ^ r) % 2
                core = (z ^ r) // 2
                for low in range(low_count):
                    pairs.append(((source * low_count + low) * 2 + core, (z * low_count + low) * 2 + t))
        slots.append(lax.ppermute(piece, ("dp", "tensor"), pairs))
    return slots


def row_parts(slots):
    rows = slots[0].shape[0]
    cut = (rows // 2 + 15) // 16 * 16
    return [jnp.stack([x[:cut] for x in slots]), jnp.stack([x[cut:] for x in slots])]


def middle_phases(parts):
    arrays, masks, last = [], [], []
    for part, held in enumerate(parts):
        order = low_masks() if part == 0 else low_masks()[::-1]
        own = [0]
        for m in order[:-1]:
            held = jnp.concatenate([held, exchange(held, m)])
            own = own + [k ^ m for k in own]
        arrays.append(held)
        masks.append(own)
        last.append(order[-1])
    return arrays, masks, last


def last_phase(arrays, masks, last):
    got = [exchange(x, m) for x, m in zip(arrays, last)]
    entries, begin = [], 0
    for part, held in enumerate(arrays):
        rows = held.shape[1]
        for number, flip in ((part, 0), (part + 2, last[part])):
            for slot in range(held.shape[0]):
                entries.append((number, slot, masks[part][slot // 4] ^ flip, slot % 4, begin, rows))
        begin += rows
    return got, tuple(entries)


def forward(arrays, plan, normed, low_rank, mine, begin, columns):
    count = lax.axis_size("dp")
    half, step = count // 2, count // 4
    row_count, half_width = normed.shape[0], normed.shape[1] // 2
    rows = half_width // half

    def body(scalars, get, raw, outs, put, scratch):
        own_ref, theirs_ref, weight_ref = outs
        normed_ref, sems = scratch
        position, tensor_part = lax.axis_index("dp"), lax.axis_index("tensor")
        top = position // half
        start = pl.multiple_of(tensor_part * half_width, half_width)
        copies = [
            pltpu.make_async_copy(raw[-1].at[:, pl.ds(start, half_width)], normed_ref, sems.at[len(plan)])
        ]
        for number, (source, slot, mask, r, first, size) in enumerate(plan):
            block = (position ^ (mask + (r % 2) * step)) % half
            copies.append(
                pltpu.make_async_copy(
                    raw[source].at[slot],
                    weight_ref.at[top ^ (r // 2), block, pl.ds(first, size)],
                    sems.at[number],
                )
            )
        for copy in copies:
            copy.start()
        up = get(1)[row_count:, begin : begin + columns]
        extra = 2.0 * dot(get(0)[...], up, 1, 0)
        for copy in copies:
            copy.wait()
        put(2)
        theirs_ref[...] = dot(normed_ref[...], weight_ref[1 - tensor_part].reshape(half_width, columns), 1, 0)
        put(1)
        own_ref[...] = extra + dot(normed_ref[...], weight_ref[tensor_part].reshape(half_width, columns), 1, 0)
        put(0)

    partial = jax.ShapeDtypeStruct((row_count, columns), jnp.float32)
    return kernel_call(
        body,
        (low_rank, mine),
        (partial, partial, jax.ShapeDtypeStruct((2, half, rows, columns), jnp.bfloat16)),
        raw=(*arrays, normed),
        scratch=(
            pltpu.VMEM((row_count, half_width), jnp.bfloat16),
            pltpu.SemaphoreType.DMA((len(plan) + 1,)),
        ),
    )


def tile_blocks(rows, half):
    blocks = 1
    while blocks < half and (blocks * rows < 512 or blocks * rows % 128):
        blocks *= 2
    return blocks


def gradient_kernel(part_ref, weight_ref, gathered_ref, mine_ref, other_ref, scaled_ref, down_ref, out_ref):
    tensor_part = part_ref[0]
    _, blocks, rows, cut = weight_ref.shape
    size, columns = blocks * rows, gathered_ref.shape[3]
    total = dot(scaled_ref[...], down_ref[...], 0, 1)
    for ref, core in ((mine_ref, tensor_part), (other_ref, 1 - tensor_part)):
        total = total + dot(ref[:, :cut], weight_ref[core].reshape(size, cut), 1, 1)
        total = total + dot(ref[:, cut:], gathered_ref[:, core].reshape(size, columns), 1, 1)
    out_ref[...] = total.astype(out_ref.dtype)


def input_gradient(part, weight, gathered, mine, other, scaled_t, down_keep):
    _, half, rows, cut = weight.shape
    columns = gathered.shape[3]
    rank, row_count = scaled_t.shape
    blocks = tile_blocks(rows, half)
    width, steps = blocks * rows, half // blocks
    masked = pl.BlockSpec((row_count, mine.shape[1]), lambda i, part: (0, 0))
    return pl.pallas_call(
        gradient_kernel,
        grid_spec=pltpu.PrefetchScalarGridSpec(
            num_scalar_prefetch=1,
            grid=(steps,),
            in_specs=[
                pl.BlockSpec((2, blocks, rows, cut), lambda i, part: (0, i, 0, 0)),
                pl.BlockSpec((blocks, 2, rows, columns), lambda i, part: (part[0] * steps + i, 0, 0, 0)),
                masked,
                masked,
                pl.BlockSpec((rank, row_count), lambda i, part: (0, 0)),
                pl.BlockSpec((width, rank), lambda i, part: (i, 0)),
            ],
            out_specs=pl.BlockSpec((row_count, width), lambda i, part: (0, i)),
        ),
        out_shape=jax.ShapeDtypeStruct((row_count, width * steps), jnp.bfloat16),
        compiler_params=vmem_limit(56),
        cost_estimate=SHORT,
    )(part, weight, gathered, mine, other, scaled_t, down_keep)


def last_values_kernel(part_ref, weight_ref, normed_ref, low_ref, up_ref, first_ref, out_ref, total_ref):
    step = pl.program_id(0)
    blocks, _, rows, columns = weight_ref.shape
    begin = first_ref.shape[1]
    row_count = low_ref.shape[0]

    @pl.when(step == 0)
    def _():
        out_ref[:, :begin] = first_ref[...]
        total_ref[...] = 2.0 * dot(low_ref[...], up_ref[row_count:, begin:], 1, 0)

    total_ref[...] += dot(normed_ref[...], weight_ref[...].reshape(blocks * rows, columns), 1, 0)

    @pl.when(step == pl.num_programs(0) - 1)
    def _():
        out_ref[:, begin:] = total_ref[...].astype(out_ref.dtype)


def last_values(part, gathered, normed, low_rank, mine, first):
    count, _, rows, columns = gathered.shape
    row_count = normed.shape[0]
    blocks = 2 * tile_blocks(rows, count // 2)
    width = blocks * rows

    def whole(x):
        return pl.BlockSpec(x.shape, lambda i, part: (0, 0))

    return pl.pallas_call(
        last_values_kernel,
        grid_spec=pltpu.PrefetchScalarGridSpec(
            num_scalar_prefetch=1,
            grid=(count // blocks,),
            in_specs=[
                pl.BlockSpec((blocks, 1, rows, columns), lambda i, part: (i, part[0], 0, 0)),
                pl.BlockSpec((row_count, width), lambda i, part: (0, i)),
                whole(low_rank),
                whole(mine),
                whole(first),
            ],
            out_specs=pl.BlockSpec((row_count, first.shape[1] + columns), lambda i, part: (0, 0)),
            scratch_shapes=[pltpu.VMEM((row_count, columns), jnp.float32)],
        ),
        out_shape=jax.ShapeDtypeStruct((row_count, first.shape[1] + columns), jnp.bfloat16),
        compiler_params=vmem_limit(56),
        cost_estimate=SHORT,
    )(part, gathered, normed, low_rank, mine, first)


def prepare_kernel(
    devices_ref, adapter_ref, valid_ref, down_hbm, up_hbm, cotangent_hbm,
    mine_ref, shared_ref, *refs,
):
    block_refs, (ids_ref, down_ref, cotangent_ref, sems) = refs[:-4], refs[-4:]
    count = lax.axis_size("dp")
    position = lax.axis_index("dp")
    tenant_count = devices_ref.shape[0]
    row_count, width = cotangent_ref.shape
    rank = mine_ref.shape[0] - row_count
    half_rows, total = down_ref.shape
    quarter = half_rows // 2
    low_count = count // 4
    base = pl.multiple_of(lax.axis_index("tensor") * half_rows, half_rows)
    load_cotangent = pltpu.make_async_copy(cotangent_hbm, cotangent_ref, sems.at[0])
    load_down = pltpu.make_async_copy(down_hbm.at[pl.ds(base, half_rows)], down_ref, sems.at[1])
    load_cotangent.start()
    load_down.start()
    zero = jnp.int32(0)
    end, own_id, first, valid, devices = zero, zero, zero, zero, zero
    ids = [zero] * count
    for slot in range(tenant_count):
        start = end
        end = end + devices_ref[slot]
        adapter = adapter_ref[slot]
        mine = jnp.logical_and(start <= position, position < end)
        own_id = jnp.where(mine, adapter, own_id)
        first = jnp.where(mine, start, first)
        valid = jnp.where(mine, valid_ref[slot], valid)
        devices = jnp.where(mine, devices_ref[slot], devices)
        for i in range(count):
            ids[i] = jnp.where(jnp.logical_and(start <= i, i < end), adapter, ids[i])
    for i in range(count):
        ids_ref[i] = ids[i]
    load_up = pltpu.make_async_copy(up_hbm.at[own_id], mine_ref.at[pl.ds(row_count, rank)], sems.at[2])
    load_up.start()
    shared_ref[0] = (devices > 1).astype(jnp.int32)
    rows = lax.broadcasted_iota(jnp.int32, (row_count, width), 0)
    keep = (position - first) * row_count + rows < valid
    load_cotangent.wait()
    mine_ref[:row_count, :] = jnp.where(keep, cotangent_ref[...], jnp.zeros_like(cotangent_ref[...]))
    load_down.wait()
    upper, lower = down_ref[0:quarter, :], down_ref[quarter:half_rows, :]
    source = lax.broadcasted_iota(jnp.int32, (total, 2 * rank), 0)
    lane = lax.broadcasted_iota(jnp.int32, (total, 2 * rank), 1) % rank
    first_side = lax.broadcasted_iota(jnp.int32, (quarter, 2 * rank), 1) < rank
    for m in range(count):
        chosen = (source == ids_ref[position ^ m] * rank + lane).astype(jnp.float32).astype(jnp.bfloat16)
        block = jnp.where(first_side, dot(upper, chosen, 1, 0), dot(lower, chosen, 1, 0))
        block_refs[m % low_count][m // low_count] = block.astype(jnp.bfloat16)
    load_up.wait()


def prepare(devices, adapter_of, valid, down_maps, up_maps, cotangent, count):
    rows, total = down_maps.shape
    rank = up_maps.shape[1]
    row_count, width = cotangent.shape
    return pl.pallas_call(
        prepare_kernel,
        out_shape=(
            jax.ShapeDtypeStruct((row_count + rank, width), cotangent.dtype),
            jax.ShapeDtypeStruct((1,), jnp.int32),
            *[jax.ShapeDtypeStruct((4, rows // 4, 2 * rank), down_maps.dtype)] * (count // 4),
        ),
        in_specs=[SMEM] * 3 + [HBM] * 3,
        out_specs=[VMEM, SMEM] + [VMEM] * (count // 4),
        scratch_shapes=[
            pltpu.SMEM((count,), jnp.int32),
            pltpu.VMEM((rows // 2, total), down_maps.dtype),
            pltpu.VMEM(cotangent.shape, cotangent.dtype),
            pltpu.SemaphoreType.DMA((3,)),
        ],
        compiler_params=vmem_limit(60),
        cost_estimate=SHORT,
    )(devices, adapter_of, valid, down_maps, up_maps, cotangent)


def back(mine, other, normed):
    row_count, half_width = normed.shape[0], normed.shape[1] // 2
    rank = mine.shape[0] - row_count

    def body(scalars, get, raw, outs, put, scratch):
        scaled_ref, term_ref = outs
        normed_ref, sem = scratch
        start = pl.multiple_of(lax.axis_index("tensor") * half_width, half_width)
        load = pltpu.make_async_copy(raw[0].at[:, pl.ds(start, half_width)], normed_ref, sem)
        load.start()
        mine_ref, other_ref = get(0), get(1)
        total = dot(mine_ref[row_count:, :], mine_ref[:row_count, :], 1, 1)
        total = total + dot(other_ref[row_count:, :], other_ref[:row_count, :], 1, 1)
        scaled = (2.0 * total).astype(jnp.bfloat16)
        scaled_ref[...] = scaled
        put(0)
        load.wait()
        term_ref[...] = dot(scaled, normed_ref[...], 1, 0)
        put(1)

    return kernel_call(
        body,
        (mine, other),
        (
            jax.ShapeDtypeStruct((rank, row_count), jnp.bfloat16),
            jax.ShapeDtypeStruct((rank, half_width), jnp.float32),
        ),
        raw=(normed,),
        scratch=(pltpu.VMEM((row_count, half_width), jnp.bfloat16), pltpu.SemaphoreType.DMA),
    )


def low_rank_of(shared, own, other, mine, term_a, normed, rank, *others, pieces=4):
    row_count, model_width = normed.shape
    half_width = model_width // 2
    columns = mine.shape[1]
    count = lax.axis_size("dp")
    low_count = count // 4
    quarter = own.shape[-2]
    size = rank // low_count
    piece = model_width // pieces

    def body(scalars, get, raw, outs, put, scratch):
        low_ref, down_ref, term_ref, *part_refs = outs
        full_ref, normed_ref, total_ref, sems = scratch
        position, tensor_part = lax.axis_index("dp"), lax.axis_index("tensor")
        loads = []
        for i in range(pieces):
            lanes = pl.ds(i * piece, piece)
            loads.append(pltpu.make_async_copy(raw[0].at[:, lanes], normed_ref.at[:, lanes], sems.at[i]))
        for load in loads:
            load.start()
        for ref, part in ((get(0), tensor_part), (get(1), 1 - tensor_part)):
            for h in range(4):
                for l in range(low_count):
                    source = position ^ (h * low_count + l)
                    block = ref[h, l]
                    for side in range(2):
                        start = pl.multiple_of((source * 4 + part * 2 + side) * quarter, quarter)
                        full_ref[pl.ds(start, quarter), :] = block[:, side * rank : (side + 1) * rank]
        down_ref[...] = full_ref[pl.ds(pl.multiple_of(tensor_part * half_width, half_width), half_width), :]
        put(1)
        for i, load in enumerate(loads):
            load.wait()
            rows = slice(i * piece, (i + 1) * piece)
            product = dot(normed_ref[:, rows], full_ref[rows, :], 1, 0)
            total_ref[...] = product if i == 0 else total_ref[...] + product
        low = total_ref[...].astype(jnp.bfloat16)
        low_ref[...] = low
        put(0)
        term_ref[...] = 2.0 * dot(low, get(2)[:row_count, :], 0, 0)
        put(2)
        shared_here = scalars[0][0] > 0
        a_ref = get(3)
        for m, ref in enumerate(part_refs):
            start = pl.multiple_of(((position % low_count) ^ m) * size, size)
            ref[:, :half_width] = jnp.where(shared_here, a_ref[pl.ds(start, size), :], 0.0)
            ref[:, half_width:] = jnp.where(shared_here, term_ref[pl.ds(start, size), :], 0.0)
            put(3 + m)

    part = jax.ShapeDtypeStruct((size, half_width + columns), jnp.float32)
    result = kernel_call(
        body,
        (own, other, mine, term_a),
        (
            jax.ShapeDtypeStruct((row_count, rank), jnp.bfloat16),
            jax.ShapeDtypeStruct((half_width, rank), jnp.bfloat16),
            jax.ShapeDtypeStruct((rank, columns), jnp.float32),
            *[part] * low_count,
        ),
        scalars=(shared,),
        raw=(normed, *others),
        scratch=(
            pltpu.VMEM((model_width, rank), jnp.bfloat16),
            pltpu.VMEM((row_count, model_width), jnp.bfloat16),
            pltpu.VMEM((row_count, rank), jnp.float32),
            pltpu.SemaphoreType.DMA((pieces,)),
        ),
    )
    return result[0], result[1], result[2], result[3:]


def send_blocks_low(blocks):
    got = [blocks[0]] + [exchange(block, l) for l, block in enumerate(blocks) if l]

    def body(scalars, get, raw, outs, put, scratch):
        refs = [get(l) for l in range(len(got))]
        for h, out in enumerate(outs):
            for l, ref in enumerate(refs):
                out[l] = ref[h]
            put(h)

    shape = jax.ShapeDtypeStruct((len(got),) + got[0].shape[1:], got[0].dtype)
    return list(kernel_call(body, got, [shape] * 4))


def send_blocks_high(rows):
    return jnp.stack([rows[0]] + [exchange(row, m) for row, m in zip(rows[1:], high_masks()[1:])])


def row_sums(parts):
    total = parts[0]
    for m, part in enumerate(parts):
        if m:
            total = total + exchange(part, m)
    return total


def sum_to_strip(total):
    low_count = lax.axis_size("dp") // 4
    high = lax.axis_index("dp") // low_count
    width = total.shape[1] // 4

    def column_part(index):
        return lax.dynamic_slice_in_dim(total, index * width, width, 1)

    share = column_part(high)
    for m in range(1, 4):
        share = share + exchange(column_part(high ^ m), m * low_count)
    share = share.astype(jnp.bfloat16)
    got = [share] + [exchange(share, m * low_count) for m in range(1, 4)]
    return jnp.concatenate([pick(got, high ^ i) for i in range(4)], axis=1)


def gather_strips(strip):
    low_count = lax.axis_size("dp") // 4
    low = lax.axis_index("dp") % low_count
    got = [strip] + [exchange(strip, m) for m in range(1, low_count)]
    return jnp.concatenate([pick(got, low ^ i) for i in range(low_count)], axis=0)


def shards(
    normed,
    cotangent,
    value_weight,
    adapter_down_maps,
    adapter_up_maps,
    tenant_devices,
    adapter_of,
    valid_tokens,
):
    row_count, model_width = normed.shape
    rank = adapter_up_maps.shape[1]
    tenant_count = tenant_devices.shape[0]
    width = value_weight.shape[1]
    count = lax.axis_size("dp")
    half_width = model_width // 2
    tensor_part = lax.axis_index("tensor")
    position = lax.axis_index("dp")
    cut = width * EXCHANGED[0] // EXCHANGED[1]

    slots = first_phase(value_weight[:, :cut])
    gathered = lax.all_gather(value_weight[:, cut:], ("dp", "tensor"), axis=0)
    gathered = gathered.reshape(count, 2, value_weight.shape[0], width - cut)

    most = 9 * count // 16
    single_run = count - most == tenant_count - 1
    if value_weight.shape[0] % 64 == 0 and single_run:
        mine, shared, *blocks = prepare(
            tenant_devices, adapter_of, valid_tokens, adapter_down_maps, adapter_up_maps, cotangent, count
        )
        other = swap_cores(mine)
        scaled_t, term_a = back(mine, other, normed)
        rows = send_blocks_low(blocks)
        held, masks, last = middle_phases(row_parts(slots))
        own_blocks = send_blocks_high(rows)
        low_rank, down_keep, term_b, parts = low_rank_of(
            shared, own_blocks, swap_cores(own_blocks), mine, term_a, normed, rank
        )
        got, plan = last_phase(held, masks, last)
        strip = sum_to_strip(row_sums(parts))
        total = gather_strips(fence(strip, gathered)).astype(jnp.float32)
        grad_a = jnp.where(shared[0] > 0, total[:, :half_width], term_a)[None]
        grad_b = jnp.where(shared[0] > 0, total[:, half_width:], term_b)[None]
    else:
        slot_ends = jnp.cumsum(tenant_devices)
        tenant_slot = jnp.sum((slot_ends <= position).astype(jnp.int32))
        picker = (jnp.arange(tenant_count, dtype=jnp.int32) == tenant_slot).astype(jnp.int32)
        first_device = jnp.sum(picker * (slot_ends - tenant_devices))
        adapter_index = jnp.sum(picker * adapter_of)
        valid_count = jnp.sum(picker * valid_tokens)
        offsets = (position - first_device) * row_count + jnp.arange(row_count, dtype=jnp.int32)
        keep_rows = offsets < valid_count
        up_matrix = lax.dynamic_index_in_dim(adapter_up_maps, adapter_index, 0, keepdims=False)
        masked = jnp.where(keep_rows[:, None], cotangent, jnp.zeros_like(cotangent))
        mine = jnp.concatenate([masked, up_matrix])
        other = swap_cores(mine)
        scaled_t, term_a = back(mine, other, normed)
        down_maps = lax.all_gather(adapter_down_maps, "dp", axis=0, tiled=True)
        down_map = lax.dynamic_slice_in_dim(down_maps, adapter_index * rank, rank, 1)
        down_keep = lax.dynamic_slice_in_dim(down_map, tensor_part * half_width, half_width, 0)
        low_rank = dot(normed, down_map, 1, 0).astype(jnp.bfloat16)
        term_b = 2.0 * dot(low_rank, masked, 0, 0)
        marks = picker.astype(jnp.float32)[:, None, None]
        totals = lax.psum((marks * term_a[None], marks * term_b[None]), "dp")
        grad_a = lax.dynamic_index_in_dim(totals[0], tenant_slot, 0, keepdims=True)
        grad_b = lax.dynamic_index_in_dim(totals[1], tenant_slot, 0, keepdims=True)
        held, masks, last = middle_phases(row_parts(slots))
        got, plan = last_phase(held, masks, last)

    own, theirs, weight = forward(held + got, plan, normed, low_rank, mine, 0, cut)
    values = (own + swap_cores(theirs)).astype(jnp.bfloat16)
    part = jnp.reshape(tensor_part, (1,))
    values = last_values(part, gathered, normed, low_rank, mine, values)
    gradient = input_gradient(part, weight, gathered, mine, other, scaled_t, down_keep)
    return (values, gradient, grad_a, grad_b)


def solution(mesh):
    return jax.shard_map(
        shards,
        mesh=mesh,
        in_specs=(
            P(("groups", "dp"), None),
            P(("groups", "dp"), "tensor"),
            P("dp", "tensor"),
            P("dp", "groups"),
            P("groups", None, "tensor"),
            P("groups"),
            P("groups"),
            P("groups"),
        ),
        out_specs=(
            P(("groups", "dp"), "tensor"),
            P(("groups", "dp"), "tensor"),
            P(("groups", "dp"), None, "tensor"),
            P(("groups", "dp"), None, "tensor"),
        ),
        check_vma=False,
    )
```

```python
import functools

import jax
import jax.numpy as jnp
from jax import lax
from jax.experimental import pallas as pl
from jax.experimental.pallas import tpu as pltpu
from jax.sharding import PartitionSpec as P

EXCHANGED = (1, 2)

HBM = pl.BlockSpec(memory_space=pltpu.HBM)
VMEM = pl.BlockSpec(memory_space=pltpu.VMEM)
SMEM = pl.BlockSpec(memory_space=pltpu.SMEM)


SHORT = pl.CostEstimate(flops=1, bytes_accessed=1, transcendentals=0)


def vmem_limit(mib):
    return pltpu.CompilerParams(vmem_limit_bytes=mib * 1024 * 1024)


def dot(left, right, left_dim, right_dim):
    return lax.dot_general(
        left,
        right,
        (((left_dim,), (right_dim,)), ((), ())),
        preferred_element_type=jnp.float32,
    )


def swap_cores(x):
    n = lax.axis_size("tensor")
    return lax.ppermute(x, "tensor", [(i, n - 1 - i) for i in range(n)])


def exchange(x, mask):
    return lax.ppermute(x, "dp", [(i, i ^ mask) for i in range(lax.axis_size("dp"))])


def pick(pieces, index):
    result = pieces[0]
    for i in range(1, len(pieces)):
        result = jnp.where(index == i, pieces[i], result)
    return result


def fence(x, *others):
    def kernel(*refs):
        pass

    return pl.pallas_call(
        kernel,
        out_shape=jax.ShapeDtypeStruct(x.shape, x.dtype),
        in_specs=[HBM] * (1 + len(others)),
        out_specs=HBM,
        input_output_aliases={0: 0},
        cost_estimate=SHORT,
    )(x, *others)


def kernel_call(body, ins, outs, scalars=(), raw=(), scratch=()):
    counts = (len(scalars), len(ins), len(raw), len(outs), len(ins), len(outs), len(scratch), 1)

    def kernel(*refs):
        groups, start = [], 0
        for count in counts:
            groups.append(refs[start : start + count])
            start += count
        scalar_refs, in_hbm, raw_refs, out_hbm, in_refs, out_refs, scratch_refs, (sems,) = groups
        loads = [
            pltpu.make_async_copy(source, target, sems.at[i])
            for i, (source, target) in enumerate(zip(in_hbm, in_refs))
        ]
        for load in loads:
            load.start()
        stores = []

        def get(i):
            loads[i].wait()
            return in_refs[i]

        def put(i):
            store = pltpu.make_async_copy(out_refs[i], out_hbm[i], sems.at[len(ins) + i])
            store.start()
            stores.append(store)

        body(scalar_refs, get, raw_refs, out_refs, put, scratch_refs)
        for store in stores:
            store.wait()

    return pl.pallas_call(
        kernel,
        out_shape=tuple(outs),
        in_specs=[SMEM] * len(scalars) + [HBM] * (len(ins) + len(raw)),
        out_specs=tuple([HBM] * len(outs)),
        scratch_shapes=[
            *[pltpu.VMEM(x.shape, x.dtype) for x in (*ins, *outs)],
            *scratch,
            pltpu.SemaphoreType.DMA((len(ins) + len(outs),)),
        ],
        compiler_params=vmem_limit(56),
        cost_estimate=SHORT,
    )(*scalars, *ins, *raw)


def high_masks():
    step = lax.axis_size("dp") // 4
    return (0, step, 2 * step, 3 * step)


def low_masks():
    masks, mask = [], 1
    while mask < lax.axis_size("dp") // 4:
        masks.append(mask)
        mask *= 2
    return masks


def first_phase(piece):
    low_count = lax.axis_size("dp") // 4
    slots = []
    for r in range(4):
        pairs = []
        for z in range(4):
            for t in range(2):
                source = 2 * t + (z ^ r) % 2
                core = (z ^ r) // 2
                for low in range(low_count):
                    pairs.append(((source * low_count + low) * 2 + core, (z * low_count + low) * 2 + t))
        slots.append(lax.ppermute(piece, ("dp", "tensor"), pairs))
    return slots


def row_parts(slots):
    rows = slots[0].shape[0]
    cut = (rows // 2 + 15) // 16 * 16
    return [jnp.stack([x[:cut] for x in slots]), jnp.stack([x[cut:] for x in slots])]


def middle_phases(parts):
    arrays, masks, last = [], [], []
    for part, held in enumerate(parts):
        order = low_masks() if part == 0 else low_masks()[::-1]
        own = [0]
        for m in order[:-1]:
            held = jnp.concatenate([held, exchange(held, m)])
            own = own + [k ^ m for k in own]
        arrays.append(held)
        masks.append(own)
        last.append(order[-1])
    return arrays, masks, last


def last_phase(arrays, masks, last):
    got = [exchange(x, m) for x, m in zip(arrays, last)]
    entries, begin = [], 0
    for part, held in enumerate(arrays):
        rows = held.shape[1]
        for number, flip in ((part, 0), (part + 2, last[part])):
            for slot in range(held.shape[0]):
                entries.append((number, slot, masks[part][slot // 4] ^ flip, slot % 4, begin, rows))
        begin += rows
    return got, tuple(entries)


def forward(arrays, plan, normed, low_rank, mine, begin, columns):
    count = lax.axis_size("dp")
    half, step = count // 2, count // 4
    row_count, half_width = normed.shape[0], normed.shape[1] // 2
    rows = half_width // half

    def body(scalars, get, raw, outs, put, scratch):
        own_ref, theirs_ref, weight_ref = outs
        normed_ref, sems = scratch
        position, tensor_part = lax.axis_index("dp"), lax.axis_index("tensor")
        top = position // half
        start = pl.multiple_of(tensor_part * half_width, half_width)
        copies = [
            pltpu.make_async_copy(raw[-1].at[:, pl.ds(start, half_width)], normed_ref, sems.at[len(plan)])
        ]
        for number, (source, slot, mask, r, first, size) in enumerate(plan):
            block = (position ^ (mask + (r % 2) * step)) % half
            copies.append(
                pltpu.make_async_copy(
                    raw[source].at[slot],
                    weight_ref.at[top ^ (r // 2), block, pl.ds(first, size)],
                    sems.at[number],
                )
            )
        for copy in copies:
            copy.start()
        up = get(1)[row_count:, begin : begin + columns]
        extra = 2.0 * dot(get(0)[...], up, 1, 0)
        for copy in copies:
            copy.wait()
        put(2)
        theirs_ref[...] = dot(normed_ref[...], weight_ref[1 - tensor_part].reshape(half_width, columns), 1, 0)
        put(1)
        own_ref[...] = extra + dot(normed_ref[...], weight_ref[tensor_part].reshape(half_width, columns), 1, 0)
        put(0)

    partial = jax.ShapeDtypeStruct((row_count, columns), jnp.float32)
    return kernel_call(
        body,
        (low_rank, mine),
        (partial, partial, jax.ShapeDtypeStruct((2, half, rows, columns), jnp.bfloat16)),
        raw=(*arrays, normed),
        scratch=(
            pltpu.VMEM((row_count, half_width), jnp.bfloat16),
            pltpu.SemaphoreType.DMA((len(plan) + 1,)),
        ),
    )


def tile_blocks(rows, half):
    blocks = 1
    while blocks < half and (blocks * rows < 512 or blocks * rows % 128):
        blocks *= 2
    return blocks


def gradient_kernel(part_ref, weight_ref, gathered_ref, mine_ref, other_ref, scaled_ref, down_ref, out_ref):
    tensor_part = part_ref[0]
    _, blocks, rows, cut = weight_ref.shape
    size, columns = blocks * rows, gathered_ref.shape[3]
    total = dot(scaled_ref[...], down_ref[...], 0, 1)
    for ref, core in ((mine_ref, tensor_part), (other_ref, 1 - tensor_part)):
        total = total + dot(ref[:, :cut], weight_ref[core].reshape(size, cut), 1, 1)
        total = total + dot(ref[:, cut:], gathered_ref[:, core].reshape(size, columns), 1, 1)
    out_ref[...] = total.astype(out_ref.dtype)


def input_gradient(part, weight, gathered, mine, other, scaled_t, down_keep):
    _, half, rows, cut = weight.shape
    columns = gathered.shape[3]
    rank, row_count = scaled_t.shape
    blocks = 2 * tile_blocks(rows, half)
    width, steps = blocks * rows, half // blocks
    masked = pl.BlockSpec((row_count, mine.shape[1]), lambda i, part: (0, 0))
    return pl.pallas_call(
        gradient_kernel,
        grid_spec=pltpu.PrefetchScalarGridSpec(
            num_scalar_prefetch=1,
            grid=(steps,),
            in_specs=[
                pl.BlockSpec((2, blocks, rows, cut), lambda i, part: (0, i, 0, 0)),
                pl.BlockSpec((blocks, 2, rows, columns), lambda i, part: (part[0] * steps + i, 0, 0, 0)),
                masked,
                masked,
                pl.BlockSpec((rank, row_count), lambda i, part: (0, 0)),
                pl.BlockSpec((width, rank), lambda i, part: (i, 0)),
            ],
            out_specs=pl.BlockSpec((row_count, width), lambda i, part: (0, i)),
        ),
        out_shape=jax.ShapeDtypeStruct((row_count, width * steps), jnp.bfloat16),
        compiler_params=vmem_limit(56),
        cost_estimate=SHORT,
    )(part, weight, gathered, mine, other, scaled_t, down_keep)


def last_values_kernel(part_ref, weight_ref, normed_ref, low_ref, up_ref, first_ref, out_ref, total_ref):
    step = pl.program_id(0)
    blocks, _, rows, columns = weight_ref.shape
    begin = first_ref.shape[1]
    row_count = low_ref.shape[0]

    @pl.when(step == 0)
    def _():
        out_ref[:, :begin] = first_ref[...]
        total_ref[...] = 2.0 * dot(low_ref[...], up_ref[row_count:, begin:], 1, 0)

    total_ref[...] += dot(normed_ref[...], weight_ref[...].reshape(blocks * rows, columns), 1, 0)

    @pl.when(step == pl.num_programs(0) - 1)
    def _():
        out_ref[:, begin:] = total_ref[...].astype(out_ref.dtype)


def last_values(part, gathered, normed, low_rank, mine, first):
    count, _, rows, columns = gathered.shape
    row_count = normed.shape[0]
    blocks = 4 * tile_blocks(rows, count // 2)
    width = blocks * rows

    def whole(x):
        return pl.BlockSpec(x.shape, lambda i, part: (0, 0))

    return pl.pallas_call(
        last_values_kernel,
        grid_spec=pltpu.PrefetchScalarGridSpec(
            num_scalar_prefetch=1,
            grid=(count // blocks,),
            in_specs=[
                pl.BlockSpec((blocks, 1, rows, columns), lambda i, part: (i, part[0], 0, 0)),
                pl.BlockSpec((row_count, width), lambda i, part: (0, i)),
                whole(low_rank),
                whole(mine),
                whole(first),
            ],
            out_specs=pl.BlockSpec((row_count, first.shape[1] + columns), lambda i, part: (0, 0)),
            scratch_shapes=[pltpu.VMEM((row_count, columns), jnp.float32)],
        ),
        out_shape=jax.ShapeDtypeStruct((row_count, first.shape[1] + columns), jnp.bfloat16),
        compiler_params=vmem_limit(56),
        cost_estimate=SHORT,
    )(part, gathered, normed, low_rank, mine, first)


def prepare_kernel(
    devices_ref, adapter_ref, valid_ref, down_hbm, up_hbm, cotangent_hbm,
    mine_ref, shared_ref, *refs,
):
    block_refs, (ids_ref, down_ref, cotangent_ref, sems) = refs[:-4], refs[-4:]
    count = lax.axis_size("dp")
    position = lax.axis_index("dp")
    tenant_count = devices_ref.shape[0]
    row_count, width = cotangent_ref.shape
    rank = mine_ref.shape[0] - row_count
    half_rows, total = down_ref.shape
    quarter = half_rows // 2
    low_count = count // 4
    base = pl.multiple_of(lax.axis_index("tensor") * half_rows, half_rows)
    load_cotangent = pltpu.make_async_copy(cotangent_hbm, cotangent_ref, sems.at[0])
    load_down = pltpu.make_async_copy(down_hbm.at[pl.ds(base, half_rows)], down_ref, sems.at[1])
    load_cotangent.start()
    load_down.start()
    zero = jnp.int32(0)
    end, own_id, first, valid, devices = zero, zero, zero, zero, zero
    ids = [zero] * count
    for slot in range(tenant_count):
        start = end
        end = end + devices_ref[slot]
        adapter = adapter_ref[slot]
        mine = jnp.logical_and(start <= position, position < end)
        own_id = jnp.where(mine, adapter, own_id)
        first = jnp.where(mine, start, first)
        valid = jnp.where(mine, valid_ref[slot], valid)
        devices = jnp.where(mine, devices_ref[slot], devices)
        for i in range(count):
            ids[i] = jnp.where(jnp.logical_and(start <= i, i < end), adapter, ids[i])
    for i in range(count):
        ids_ref[i] = ids[i]
    load_up = pltpu.make_async_copy(up_hbm.at[own_id], mine_ref.at[pl.ds(row_count, rank)], sems.at[2])
    load_up.start()
    shared_ref[0] = (devices > 1).astype(jnp.int32)
    rows = lax.broadcasted_iota(jnp.int32, (row_count, width), 0)
    keep = (position - first) * row_count + rows < valid
    load_cotangent.wait()
    mine_ref[:row_count, :] = jnp.where(keep, cotangent_ref[...], jnp.zeros_like(cotangent_ref[...]))
    load_down.wait()
    upper, lower = down_ref[0:quarter, :], down_ref[quarter:half_rows, :]
    source = lax.broadcasted_iota(jnp.int32, (total, 2 * rank), 0)
    lane = lax.broadcasted_iota(jnp.int32, (total, 2 * rank), 1) % rank
    first_side = lax.broadcasted_iota(jnp.int32, (quarter, 2 * rank), 1) < rank
    for m in range(count):
        chosen = (source == ids_ref[position ^ m] * rank + lane).astype(jnp.float32).astype(jnp.bfloat16)
        block = jnp.where(first_side, dot(upper, chosen, 1, 0), dot(lower, chosen, 1, 0))
        block_refs[m % low_count][m // low_count] = block.astype(jnp.bfloat16)
    load_up.wait()


def prepare(devices, adapter_of, valid, down_maps, up_maps, cotangent, count):
    rows, total = down_maps.shape
    rank = up_maps.shape[1]
    row_count, width = cotangent.shape
    return pl.pallas_call(
        prepare_kernel,
        out_shape=(
            jax.ShapeDtypeStruct((row_count + rank, width), cotangent.dtype),
            jax.ShapeDtypeStruct((1,), jnp.int32),
            *[jax.ShapeDtypeStruct((4, rows // 4, 2 * rank), down_maps.dtype)] * (count // 4),
        ),
        in_specs=[SMEM] * 3 + [HBM] * 3,
        out_specs=[VMEM, SMEM] + [VMEM] * (count // 4),
        scratch_shapes=[
            pltpu.SMEM((count,), jnp.int32),
            pltpu.VMEM((rows // 2, total), down_maps.dtype),
            pltpu.VMEM(cotangent.shape, cotangent.dtype),
            pltpu.SemaphoreType.DMA((3,)),
        ],
        compiler_params=vmem_limit(60),
        cost_estimate=SHORT,
    )(devices, adapter_of, valid, down_maps, up_maps, cotangent)


def back(mine, other, normed):
    row_count, half_width = normed.shape[0], normed.shape[1] // 2
    rank = mine.shape[0] - row_count

    def body(scalars, get, raw, outs, put, scratch):
        scaled_ref, term_ref = outs
        normed_ref, sem = scratch
        start = pl.multiple_of(lax.axis_index("tensor") * half_width, half_width)
        load = pltpu.make_async_copy(raw[0].at[:, pl.ds(start, half_width)], normed_ref, sem)
        load.start()
        mine_ref, other_ref = get(0), get(1)
        total = dot(mine_ref[row_count:, :], mine_ref[:row_count, :], 1, 1)
        total = total + dot(other_ref[row_count:, :], other_ref[:row_count, :], 1, 1)
        scaled = (2.0 * total).astype(jnp.bfloat16)
        scaled_ref[...] = scaled
        put(0)
        load.wait()
        term_ref[...] = dot(scaled, normed_ref[...], 1, 0)
        put(1)

    return kernel_call(
        body,
        (mine, other),
        (
            jax.ShapeDtypeStruct((rank, row_count), jnp.bfloat16),
            jax.ShapeDtypeStruct((rank, half_width), jnp.float32),
        ),
        raw=(normed,),
        scratch=(pltpu.VMEM((row_count, half_width), jnp.bfloat16), pltpu.SemaphoreType.DMA),
    )


def low_rank_of(shared, own, other, mine, term_a, normed, rank, *others, pieces=4):
    row_count, model_width = normed.shape
    half_width = model_width // 2
    columns = mine.shape[1]
    count = lax.axis_size("dp")
    low_count = count // 4
    quarter = own.shape[-2]
    size = rank // low_count
    piece = model_width // pieces

    def body(scalars, get, raw, outs, put, scratch):
        low_ref, down_ref, term_ref, *part_refs = outs
        full_ref, normed_ref, total_ref, sems = scratch
        position, tensor_part = lax.axis_index("dp"), lax.axis_index("tensor")
        loads = []
        for i in range(pieces):
            lanes = pl.ds(i * piece, piece)
            loads.append(pltpu.make_async_copy(raw[0].at[:, lanes], normed_ref.at[:, lanes], sems.at[i]))
        for load in loads:
            load.start()
        for ref, part in ((get(0), tensor_part), (get(1), 1 - tensor_part)):
            for h in range(4):
                for l in range(low_count):
                    source = position ^ (h * low_count + l)
                    block = ref[h, l]
                    for side in range(2):
                        start = pl.multiple_of((source * 4 + part * 2 + side) * quarter, quarter)
                        full_ref[pl.ds(start, quarter), :] = block[:, side * rank : (side + 1) * rank]
        down_ref[...] = full_ref[pl.ds(pl.multiple_of(tensor_part * half_width, half_width), half_width), :]
        put(1)
        for i, load in enumerate(loads):
            load.wait()
            rows = slice(i * piece, (i + 1) * piece)
            product = dot(normed_ref[:, rows], full_ref[rows, :], 1, 0)
            total_ref[...] = product if i == 0 else total_ref[...] + product
        low = total_ref[...].astype(jnp.bfloat16)
        low_ref[...] = low
        put(0)
        term_ref[...] = 2.0 * dot(low, get(2)[:row_count, :], 0, 0)
        put(2)
        shared_here = scalars[0][0] > 0
        a_ref = get(3)
        for m, ref in enumerate(part_refs):
            start = pl.multiple_of(((position % low_count) ^ m) * size, size)
            ref[:, :half_width] = jnp.where(shared_here, a_ref[pl.ds(start, size), :], 0.0)
            ref[:, half_width:] = jnp.where(shared_here, term_ref[pl.ds(start, size), :], 0.0)
            put(3 + m)

    part = jax.ShapeDtypeStruct((size, half_width + columns), jnp.float32)
    result = kernel_call(
        body,
        (own, other, mine, term_a),
        (
            jax.ShapeDtypeStruct((row_count, rank), jnp.bfloat16),
            jax.ShapeDtypeStruct((half_width, rank), jnp.bfloat16),
            jax.ShapeDtypeStruct((rank, columns), jnp.float32),
            *[part] * low_count,
        ),
        scalars=(shared,),
        raw=(normed, *others),
        scratch=(
            pltpu.VMEM((model_width, rank), jnp.bfloat16),
            pltpu.VMEM((row_count, model_width), jnp.bfloat16),
            pltpu.VMEM((row_count, rank), jnp.float32),
            pltpu.SemaphoreType.DMA((pieces,)),
        ),
    )
    return result[0], result[1], result[2], result[3:]


def send_blocks_low(blocks):
    got = [blocks[0]] + [exchange(block, l) for l, block in enumerate(blocks) if l]

    def body(scalars, get, raw, outs, put, scratch):
        refs = [get(l) for l in range(len(got))]
        for h, out in enumerate(outs):
            for l, ref in enumerate(refs):
                out[l] = ref[h]
            put(h)

    shape = jax.ShapeDtypeStruct((len(got),) + got[0].shape[1:], got[0].dtype)
    return list(kernel_call(body, got, [shape] * 4))


def send_blocks_high(rows):
    return jnp.stack([rows[0]] + [exchange(row, m) for row, m in zip(rows[1:], high_masks()[1:])])


def row_sums(parts):
    total = parts[0]
    for m, part in enumerate(parts):
        if m:
            total = total + exchange(part, m)
    return total


def sum_to_strip(total):
    low_count = lax.axis_size("dp") // 4
    high = lax.axis_index("dp") // low_count
    width = total.shape[1] // 4

    def column_part(index):
        return lax.dynamic_slice_in_dim(total, index * width, width, 1)

    share = column_part(high)
    for m in range(1, 4):
        share = share + exchange(column_part(high ^ m), m * low_count)
    share = share.astype(jnp.bfloat16)
    got = [share] + [exchange(share, m * low_count) for m in range(1, 4)]
    return jnp.concatenate([pick(got, high ^ i) for i in range(4)], axis=1)


def gather_strips(strip):
    low_count = lax.axis_size("dp") // 4
    low = lax.axis_index("dp") % low_count
    got = [strip] + [exchange(strip, m) for m in range(1, low_count)]
    return jnp.concatenate([pick(got, low ^ i) for i in range(low_count)], axis=0)


def shards(
    normed,
    cotangent,
    value_weight,
    adapter_down_maps,
    adapter_up_maps,
    tenant_devices,
    adapter_of,
    valid_tokens,
):
    row_count, model_width = normed.shape
    rank = adapter_up_maps.shape[1]
    tenant_count = tenant_devices.shape[0]
    width = value_weight.shape[1]
    count = lax.axis_size("dp")
    half_width = model_width // 2
    tensor_part = lax.axis_index("tensor")
    position = lax.axis_index("dp")
    cut = width * EXCHANGED[0] // EXCHANGED[1]

    slots = first_phase(value_weight[:, :cut])
    gathered = lax.all_gather(value_weight[:, cut:], ("dp", "tensor"), axis=0)
    gathered = gathered.reshape(count, 2, value_weight.shape[0], width - cut)

    most = 9 * count // 16
    single_run = count - most == tenant_count - 1
    if value_weight.shape[0] % 64 == 0 and single_run:
        mine, shared, *blocks = prepare(
            tenant_devices, adapter_of, valid_tokens, adapter_down_maps, adapter_up_maps, cotangent, count
        )
        other = swap_cores(mine)
        scaled_t, term_a = back(mine, other, normed)
        rows = send_blocks_low(blocks)
        held, masks, last = middle_phases(row_parts(slots))
        own_blocks = send_blocks_high(rows)
        low_rank, down_keep, term_b, parts = low_rank_of(
            shared, own_blocks, swap_cores(own_blocks), mine, term_a, normed, rank
        )
        got, plan = last_phase(held, masks, last)
        strip = sum_to_strip(row_sums(parts))
        total = gather_strips(fence(strip, gathered)).astype(jnp.float32)
        grad_a = jnp.where(shared[0] > 0, total[:, :half_width], term_a)[None]
        grad_b = jnp.where(shared[0] > 0, total[:, half_width:], term_b)[None]
    else:
        slot_ends = jnp.cumsum(tenant_devices)
        tenant_slot = jnp.sum((slot_ends <= position).astype(jnp.int32))
        picker = (jnp.arange(tenant_count, dtype=jnp.int32) == tenant_slot).astype(jnp.int32)
        first_device = jnp.sum(picker * (slot_ends - tenant_devices))
        adapter_index = jnp.sum(picker * adapter_of)
        valid_count = jnp.sum(picker * valid_tokens)
        offsets = (position - first_device) * row_count + jnp.arange(row_count, dtype=jnp.int32)
        keep_rows = offsets < valid_count
        up_matrix = lax.dynamic_index_in_dim(adapter_up_maps, adapter_index, 0, keepdims=False)
        masked = jnp.where(keep_rows[:, None], cotangent, jnp.zeros_like(cotangent))
        mine = jnp.concatenate([masked, up_matrix])
        other = swap_cores(mine)
        scaled_t, term_a = back(mine, other, normed)
        down_maps = lax.all_gather(adapter_down_maps, "dp", axis=0, tiled=True)
        down_map = lax.dynamic_slice_in_dim(down_maps, adapter_index * rank, rank, 1)
        down_keep = lax.dynamic_slice_in_dim(down_map, tensor_part * half_width, half_width, 0)
        low_rank = dot(normed, down_map, 1, 0).astype(jnp.bfloat16)
        term_b = 2.0 * dot(low_rank, masked, 0, 0)
        marks = picker.astype(jnp.float32)[:, None, None]
        totals = lax.psum((marks * term_a[None], marks * term_b[None]), "dp")
        grad_a = lax.dynamic_index_in_dim(totals[0], tenant_slot, 0, keepdims=True)
        grad_b = lax.dynamic_index_in_dim(totals[1], tenant_slot, 0, keepdims=True)
        held, masks, last = middle_phases(row_parts(slots))
        got, plan = last_phase(held, masks, last)

    own, theirs, weight = forward(held + got, plan, normed, low_rank, mine, 0, cut)
    values = (own + swap_cores(theirs)).astype(jnp.bfloat16)
    part = jnp.reshape(tensor_part, (1,))
    values = last_values(part, gathered, normed, low_rank, mine, values)
    gradient = input_gradient(part, weight, gathered, mine, other, scaled_t, down_keep)
    return (values, gradient, grad_a, grad_b)


def solution(mesh):
    return jax.shard_map(
        shards,
        mesh=mesh,
        in_specs=(
            P(("groups", "dp"), None),
            P(("groups", "dp"), "tensor"),
            P("dp", "tensor"),
            P("dp", "groups"),
            P("groups", None, "tensor"),
            P("groups"),
            P("groups"),
            P("groups"),
        ),
        out_specs=(
            P(("groups", "dp"), "tensor"),
            P(("groups", "dp"), "tensor"),
            P(("groups", "dp"), None, "tensor"),
            P(("groups", "dp"), None, "tensor"),
        ),
        check_vma=False,
    )
```

```python
import functools

import jax
import jax.numpy as jnp
from jax import lax
from jax.experimental import pallas as pl
from jax.experimental.pallas import tpu as pltpu
from jax.sharding import PartitionSpec as P

EXCHANGED = (1, 2)

HBM = pl.BlockSpec(memory_space=pltpu.HBM)
VMEM = pl.BlockSpec(memory_space=pltpu.VMEM)
SMEM = pl.BlockSpec(memory_space=pltpu.SMEM)


SHORT = pl.CostEstimate(flops=1, bytes_accessed=1, transcendentals=0)


def vmem_limit(mib):
    return pltpu.CompilerParams(vmem_limit_bytes=mib * 1024 * 1024)


def dot(left, right, left_dim, right_dim):
    return lax.dot_general(
        left,
        right,
        (((left_dim,), (right_dim,)), ((), ())),
        preferred_element_type=jnp.float32,
    )


def swap_cores(x):
    n = lax.axis_size("tensor")
    return lax.ppermute(x, "tensor", [(i, n - 1 - i) for i in range(n)])


def exchange(x, mask):
    return lax.ppermute(x, "dp", [(i, i ^ mask) for i in range(lax.axis_size("dp"))])


def pick(pieces, index):
    result = pieces[0]
    for i in range(1, len(pieces)):
        result = jnp.where(index == i, pieces[i], result)
    return result


def fence(x, *others):
    def kernel(*refs):
        pass

    return pl.pallas_call(
        kernel,
        out_shape=jax.ShapeDtypeStruct(x.shape, x.dtype),
        in_specs=[HBM] * (1 + len(others)),
        out_specs=HBM,
        input_output_aliases={0: 0},
        cost_estimate=SHORT,
    )(x, *others)


def kernel_call(body, ins, outs, scalars=(), raw=(), scratch=()):
    counts = (len(scalars), len(ins), len(raw), len(outs), len(ins), len(outs), len(scratch), 1)

    def kernel(*refs):
        groups, start = [], 0
        for count in counts:
            groups.append(refs[start : start + count])
            start += count
        scalar_refs, in_hbm, raw_refs, out_hbm, in_refs, out_refs, scratch_refs, (sems,) = groups
        loads = [
            pltpu.make_async_copy(source, target, sems.at[i])
            for i, (source, target) in enumerate(zip(in_hbm, in_refs))
        ]
        for load in loads:
            load.start()
        stores = []

        def get(i):
            loads[i].wait()
            return in_refs[i]

        def put(i):
            store = pltpu.make_async_copy(out_refs[i], out_hbm[i], sems.at[len(ins) + i])
            store.start()
            stores.append(store)

        body(scalar_refs, get, raw_refs, out_refs, put, scratch_refs)
        for store in stores:
            store.wait()

    return pl.pallas_call(
        kernel,
        out_shape=tuple(outs),
        in_specs=[SMEM] * len(scalars) + [HBM] * (len(ins) + len(raw)),
        out_specs=tuple([HBM] * len(outs)),
        scratch_shapes=[
            *[pltpu.VMEM(x.shape, x.dtype) for x in (*ins, *outs)],
            *scratch,
            pltpu.SemaphoreType.DMA((len(ins) + len(outs),)),
        ],
        compiler_params=vmem_limit(56),
        cost_estimate=SHORT,
    )(*scalars, *ins, *raw)


def high_masks():
    step = lax.axis_size("dp") // 4
    return (0, step, 2 * step, 3 * step)


def low_masks():
    masks, mask = [], 1
    while mask < lax.axis_size("dp") // 4:
        masks.append(mask)
        mask *= 2
    return masks


def first_phase(piece):
    low_count = lax.axis_size("dp") // 4
    slots = []
    for r in range(4):
        pairs = []
        for z in range(4):
            for t in range(2):
                source = 2 * t + (z ^ r) % 2
                core = (z ^ r) // 2
                for low in range(low_count):
                    pairs.append(((source * low_count + low) * 2 + core, (z * low_count + low) * 2 + t))
        slots.append(lax.ppermute(piece, ("dp", "tensor"), pairs))
    return slots


def row_parts(slots):
    rows = slots[0].shape[0]
    cut = (rows // 2 + 15) // 16 * 16
    return [jnp.stack([x[:cut] for x in slots]), jnp.stack([x[cut:] for x in slots])]


def middle_phases(parts):
    arrays, masks, last = [], [], []
    for part, held in enumerate(parts):
        order = low_masks() if part == 0 else low_masks()[::-1]
        own = [0]
        for m in order[:-1]:
            held = jnp.concatenate([held, exchange(held, m)])
            own = own + [k ^ m for k in own]
        arrays.append(held)
        masks.append(own)
        last.append(order[-1])
    return arrays, masks, last


def last_phase(arrays, masks, last):
    got = [exchange(x, m) for x, m in zip(arrays, last)]
    entries, begin = [], 0
    for part, held in enumerate(arrays):
        rows = held.shape[1]
        for number, flip in ((part, 0), (part + 2, last[part])):
            for slot in range(held.shape[0]):
                entries.append((number, slot, masks[part][slot // 4] ^ flip, slot % 4, begin, rows))
        begin += rows
    return got, tuple(entries)


def forward(arrays, plan, normed, low_rank, mine, begin, columns):
    count = lax.axis_size("dp")
    half, step = count // 2, count // 4
    row_count, half_width = normed.shape[0], normed.shape[1] // 2
    rows = half_width // half

    def body(scalars, get, raw, outs, put, scratch):
        own_ref, theirs_ref, weight_ref = outs
        normed_ref, sems = scratch
        position, tensor_part = lax.axis_index("dp"), lax.axis_index("tensor")
        top = position // half
        start = pl.multiple_of(tensor_part * half_width, half_width)
        copies = [
            pltpu.make_async_copy(raw[-1].at[:, pl.ds(start, half_width)], normed_ref, sems.at[len(plan)])
        ]
        for number, (source, slot, mask, r, first, size) in enumerate(plan):
            block = (position ^ (mask + (r % 2) * step)) % half
            copies.append(
                pltpu.make_async_copy(
                    raw[source].at[slot],
                    weight_ref.at[top ^ (r // 2), block, pl.ds(first, size)],
                    sems.at[number],
                )
            )
        for copy in copies:
            copy.start()
        up = get(1)[row_count:, begin : begin + columns]
        extra = 2.0 * dot(get(0)[...], up, 1, 0)
        for copy in copies:
            copy.wait()
        put(2)
        theirs_ref[...] = dot(normed_ref[...], weight_ref[1 - tensor_part].reshape(half_width, columns), 1, 0)
        put(1)
        own_ref[...] = extra + dot(normed_ref[...], weight_ref[tensor_part].reshape(half_width, columns), 1, 0)
        put(0)

    partial = jax.ShapeDtypeStruct((row_count, columns), jnp.float32)
    return kernel_call(
        body,
        (low_rank, mine),
        (partial, partial, jax.ShapeDtypeStruct((2, half, rows, columns), jnp.bfloat16)),
        raw=(*arrays, normed),
        scratch=(
            pltpu.VMEM((row_count, half_width), jnp.bfloat16),
            pltpu.SemaphoreType.DMA((len(plan) + 1,)),
        ),
    )


def tile_blocks(rows, half):
    blocks = 1
    while blocks < half and (blocks * rows < 512 or blocks * rows % 128):
        blocks *= 2
    return blocks


def gradient_kernel(part_ref, weight_ref, gathered_ref, mine_ref, other_ref, scaled_ref, down_ref, out_ref):
    tensor_part = part_ref[0]
    _, blocks, rows, cut = weight_ref.shape
    size, columns = blocks * rows, gathered_ref.shape[3]
    total = dot(scaled_ref[...], down_ref[...], 0, 1)
    for ref, core in ((mine_ref, tensor_part), (other_ref, 1 - tensor_part)):
        total = total + dot(ref[:, :cut], weight_ref[core].reshape(size, cut), 1, 1)
        total = total + dot(ref[:, cut:], gathered_ref[:, core].reshape(size, columns), 1, 1)
    out_ref[...] = total.astype(out_ref.dtype)


def input_gradient(part, weight, gathered, mine, other, scaled_t, down_keep):
    _, half, rows, cut = weight.shape
    columns = gathered.shape[3]
    rank, row_count = scaled_t.shape
    blocks = 2 * tile_blocks(rows, half)
    width, steps = blocks * rows, half // blocks
    masked = pl.BlockSpec((row_count, mine.shape[1]), lambda i, part: (0, 0))
    return pl.pallas_call(
        gradient_kernel,
        grid_spec=pltpu.PrefetchScalarGridSpec(
            num_scalar_prefetch=1,
            grid=(steps,),
            in_specs=[
                pl.BlockSpec((2, blocks, rows, cut), lambda i, part: (0, i, 0, 0)),
                pl.BlockSpec((blocks, 2, rows, columns), lambda i, part: (part[0] * steps + i, 0, 0, 0)),
                masked,
                masked,
                pl.BlockSpec((rank, row_count), lambda i, part: (0, 0)),
                pl.BlockSpec((width, rank), lambda i, part: (i, 0)),
            ],
            out_specs=pl.BlockSpec((row_count, width), lambda i, part: (0, i)),
        ),
        out_shape=jax.ShapeDtypeStruct((row_count, width * steps), jnp.bfloat16),
        compiler_params=vmem_limit(56),
        cost_estimate=SHORT,
    )(part, weight, gathered, mine, other, scaled_t, down_keep)


def last_values_kernel(part_ref, weight_ref, normed_ref, low_ref, up_ref, own_ref, theirs_ref, out_ref, total_ref):
    step = pl.program_id(0)
    blocks, _, rows, columns = weight_ref.shape
    begin = own_ref.shape[1]

    @pl.when(step == 0)
    def _():
        out_ref[:, :begin] = (own_ref[...] + theirs_ref[...]).astype(out_ref.dtype)
        total_ref[...] = 2.0 * dot(low_ref[...], up_ref[:, begin:], 1, 0)

    total_ref[...] += dot(normed_ref[...], weight_ref[...].reshape(blocks * rows, columns), 1, 0)

    @pl.when(step == pl.num_programs(0) - 1)
    def _():
        out_ref[:, begin:] = total_ref[...].astype(out_ref.dtype)


def last_values(part, gathered, normed, low_rank, up_matrix, own, theirs):
    count, _, rows, columns = gathered.shape
    row_count = normed.shape[0]
    blocks = 4 * tile_blocks(rows, count // 2)
    width = blocks * rows

    def whole(x):
        return pl.BlockSpec(x.shape, lambda i, part: (0, 0))

    return pl.pallas_call(
        last_values_kernel,
        grid_spec=pltpu.PrefetchScalarGridSpec(
            num_scalar_prefetch=1,
            grid=(count // blocks,),
            in_specs=[
                pl.BlockSpec((blocks, 1, rows, columns), lambda i, part: (i, part[0], 0, 0)),
                pl.BlockSpec((row_count, width), lambda i, part: (0, i)),
                whole(low_rank),
                whole(up_matrix),
                whole(own),
                whole(theirs),
            ],
            out_specs=pl.BlockSpec((row_count, own.shape[1] + columns), lambda i, part: (0, 0)),
            scratch_shapes=[pltpu.VMEM((row_count, columns), jnp.float32)],
        ),
        out_shape=jax.ShapeDtypeStruct((row_count, own.shape[1] + columns), jnp.bfloat16),
        compiler_params=vmem_limit(56),
        cost_estimate=SHORT,
    )(part, gathered, normed, low_rank, up_matrix, own, theirs)


def prepare_kernel(
    devices_ref, adapter_ref, valid_ref, down_hbm, up_hbm, cotangent_hbm,
    mine_ref, shared_ref, *refs,
):
    block_refs, (ids_ref, down_ref, cotangent_ref, sems) = refs[:-4], refs[-4:]
    count = lax.axis_size("dp")
    position = lax.axis_index("dp")
    tenant_count = devices_ref.shape[0]
    row_count, width = cotangent_ref.shape
    rank = mine_ref.shape[0] - row_count
    half_rows, total = down_ref.shape
    quarter = half_rows // 2
    low_count = count // 4
    base = pl.multiple_of(lax.axis_index("tensor") * half_rows, half_rows)
    load_cotangent = pltpu.make_async_copy(cotangent_hbm, cotangent_ref, sems.at[0])
    load_down = pltpu.make_async_copy(down_hbm.at[pl.ds(base, half_rows)], down_ref, sems.at[1])
    load_cotangent.start()
    load_down.start()
    zero = jnp.int32(0)
    end, own_id, first, valid, devices = zero, zero, zero, zero, zero
    ids = [zero] * count
    for slot in range(tenant_count):
        start = end
        end = end + devices_ref[slot]
        adapter = adapter_ref[slot]
        mine = jnp.logical_and(start <= position, position < end)
        own_id = jnp.where(mine, adapter, own_id)
        first = jnp.where(mine, start, first)
        valid = jnp.where(mine, valid_ref[slot], valid)
        devices = jnp.where(mine, devices_ref[slot], devices)
        for i in range(count):
            ids[i] = jnp.where(jnp.logical_and(start <= i, i < end), adapter, ids[i])
    for i in range(count):
        ids_ref[i] = ids[i]
    load_up = pltpu.make_async_copy(up_hbm.at[own_id], mine_ref.at[pl.ds(row_count, rank)], sems.at[2])
    load_up.start()
    shared_ref[0] = (devices > 1).astype(jnp.int32)
    rows = lax.broadcasted_iota(jnp.int32, (row_count, width), 0)
    keep = (position - first) * row_count + rows < valid
    load_cotangent.wait()
    mine_ref[:row_count, :] = jnp.where(keep, cotangent_ref[...], jnp.zeros_like(cotangent_ref[...]))
    load_down.wait()
    upper, lower = down_ref[0:quarter, :], down_ref[quarter:half_rows, :]
    source = lax.broadcasted_iota(jnp.int32, (total, 2 * rank), 0)
    lane = lax.broadcasted_iota(jnp.int32, (total, 2 * rank), 1) % rank
    first_side = lax.broadcasted_iota(jnp.int32, (quarter, 2 * rank), 1) < rank
    for m in range(count):
        chosen = (source == ids_ref[position ^ m] * rank + lane).astype(jnp.float32).astype(jnp.bfloat16)
        block = jnp.where(first_side, dot(upper, chosen, 1, 0), dot(lower, chosen, 1, 0))
        block_refs[m % low_count][m // low_count] = block.astype(jnp.bfloat16)
    load_up.wait()


def prepare(devices, adapter_of, valid, down_maps, up_maps, cotangent, count):
    rows, total = down_maps.shape
    rank = up_maps.shape[1]
    row_count, width = cotangent.shape
    return pl.pallas_call(
        prepare_kernel,
        out_shape=(
            jax.ShapeDtypeStruct((row_count + rank, width), cotangent.dtype),
            jax.ShapeDtypeStruct((1,), jnp.int32),
            *[jax.ShapeDtypeStruct((4, rows // 4, 2 * rank), down_maps.dtype)] * (count // 4),
        ),
        in_specs=[SMEM] * 3 + [HBM] * 3,
        out_specs=[VMEM, SMEM] + [VMEM] * (count // 4),
        scratch_shapes=[
            pltpu.SMEM((count,), jnp.int32),
            pltpu.VMEM((rows // 2, total), down_maps.dtype),
            pltpu.VMEM(cotangent.shape, cotangent.dtype),
            pltpu.SemaphoreType.DMA((3,)),
        ],
        compiler_params=vmem_limit(60),
        cost_estimate=SHORT,
    )(devices, adapter_of, valid, down_maps, up_maps, cotangent)


def back(mine, other, normed):
    row_count, half_width = normed.shape[0], normed.shape[1] // 2
    rank = mine.shape[0] - row_count

    def body(scalars, get, raw, outs, put, scratch):
        scaled_ref, term_ref = outs
        normed_ref, sem = scratch
        start = pl.multiple_of(lax.axis_index("tensor") * half_width, half_width)
        load = pltpu.make_async_copy(raw[0].at[:, pl.ds(start, half_width)], normed_ref, sem)
        load.start()
        mine_ref, other_ref = get(0), get(1)
        total = dot(mine_ref[row_count:, :], mine_ref[:row_count, :], 1, 1)
        total = total + dot(other_ref[row_count:, :], other_ref[:row_count, :], 1, 1)
        scaled = (2.0 * total).astype(jnp.bfloat16)
        scaled_ref[...] = scaled
        put(0)
        load.wait()
        term_ref[...] = dot(scaled, normed_ref[...], 1, 0)
        put(1)

    return kernel_call(
        body,
        (mine, other),
        (
            jax.ShapeDtypeStruct((rank, row_count), jnp.bfloat16),
            jax.ShapeDtypeStruct((rank, half_width), jnp.float32),
        ),
        raw=(normed,),
        scratch=(pltpu.VMEM((row_count, half_width), jnp.bfloat16), pltpu.SemaphoreType.DMA),
    )


def low_rank_of(shared, own, other, mine, term_a, normed, rank, *others, pieces=4):
    row_count, model_width = normed.shape
    half_width = model_width // 2
    columns = mine.shape[1]
    count = lax.axis_size("dp")
    low_count = count // 4
    quarter = own.shape[-2]
    size = rank // low_count
    piece = model_width // pieces

    def body(scalars, get, raw, outs, put, scratch):
        low_ref, down_ref, term_ref, *part_refs = outs
        full_ref, normed_ref, total_ref, sems = scratch
        position, tensor_part = lax.axis_index("dp"), lax.axis_index("tensor")
        loads = []
        for i in range(pieces):
            lanes = pl.ds(i * piece, piece)
            loads.append(pltpu.make_async_copy(raw[0].at[:, lanes], normed_ref.at[:, lanes], sems.at[i]))
        for load in loads:
            load.start()
        for ref, part in ((get(0), tensor_part), (get(1), 1 - tensor_part)):
            for h in range(4):
                for l in range(low_count):
                    source = position ^ (h * low_count + l)
                    block = ref[h, l]
                    for side in range(2):
                        start = pl.multiple_of((source * 4 + part * 2 + side) * quarter, quarter)
                        full_ref[pl.ds(start, quarter), :] = block[:, side * rank : (side + 1) * rank]
        down_ref[...] = full_ref[pl.ds(pl.multiple_of(tensor_part * half_width, half_width), half_width), :]
        put(1)
        for i, load in enumerate(loads):
            load.wait()
            rows = slice(i * piece, (i + 1) * piece)
            product = dot(normed_ref[:, rows], full_ref[rows, :], 1, 0)
            total_ref[...] = product if i == 0 else total_ref[...] + product
        low = total_ref[...].astype(jnp.bfloat16)
        low_ref[...] = low
        put(0)
        term_ref[...] = 2.0 * dot(low, get(2)[:row_count, :], 0, 0)
        put(2)
        shared_here = scalars[0][0] > 0
        a_ref = get(3)
        for m, ref in enumerate(part_refs):
            start = pl.multiple_of(((position % low_count) ^ m) * size, size)
            ref[:, :half_width] = jnp.where(shared_here, a_ref[pl.ds(start, size), :], 0.0)
            ref[:, half_width:] = jnp.where(shared_here, term_ref[pl.ds(start, size), :], 0.0)
            put(3 + m)

    part = jax.ShapeDtypeStruct((size, half_width + columns), jnp.float32)
    result = kernel_call(
        body,
        (own, other, mine, term_a),
        (
            jax.ShapeDtypeStruct((row_count, rank), jnp.bfloat16),
            jax.ShapeDtypeStruct((half_width, rank), jnp.bfloat16),
            jax.ShapeDtypeStruct((rank, columns), jnp.float32),
            *[part] * low_count,
        ),
        scalars=(shared,),
        raw=(normed, *others),
        scratch=(
            pltpu.VMEM((model_width, rank), jnp.bfloat16),
            pltpu.VMEM((row_count, model_width), jnp.bfloat16),
            pltpu.VMEM((row_count, rank), jnp.float32),
            pltpu.SemaphoreType.DMA((pieces,)),
        ),
    )
    return result[0], result[1], result[2], result[3:]


def send_blocks_low(blocks):
    got = [blocks[0]] + [exchange(block, l) for l, block in enumerate(blocks) if l]

    def body(scalars, get, raw, outs, put, scratch):
        refs = [get(l) for l in range(len(got))]
        for h, out in enumerate(outs):
            for l, ref in enumerate(refs):
                out[l] = ref[h]
            put(h)

    shape = jax.ShapeDtypeStruct((len(got),) + got[0].shape[1:], got[0].dtype)
    return list(kernel_call(body, got, [shape] * 4))


def send_blocks_high(rows):
    return jnp.stack([rows[0]] + [exchange(row, m) for row, m in zip(rows[1:], high_masks()[1:])])


def row_sums(parts):
    total = parts[0]
    for m, part in enumerate(parts):
        if m:
            total = total + exchange(part, m)
    return total


def sum_to_strip(total):
    low_count = lax.axis_size("dp") // 4
    high = lax.axis_index("dp") // low_count
    width = total.shape[1] // 4

    def column_part(index):
        return lax.dynamic_slice_in_dim(total, index * width, width, 1)

    share = column_part(high)
    for m in range(1, 4):
        share = share + exchange(column_part(high ^ m), m * low_count)
    share = share.astype(jnp.bfloat16)
    got = [share] + [exchange(share, m * low_count) for m in range(1, 4)]
    return jnp.concatenate([pick(got, high ^ i) for i in range(4)], axis=1)


def gather_strips(strip):
    low_count = lax.axis_size("dp") // 4
    low = lax.axis_index("dp") % low_count
    got = [strip] + [exchange(strip, m) for m in range(1, low_count)]
    return jnp.concatenate([pick(got, low ^ i) for i in range(low_count)], axis=0)


def shards(
    normed,
    cotangent,
    value_weight,
    adapter_down_maps,
    adapter_up_maps,
    tenant_devices,
    adapter_of,
    valid_tokens,
):
    row_count, model_width = normed.shape
    rank = adapter_up_maps.shape[1]
    tenant_count = tenant_devices.shape[0]
    width = value_weight.shape[1]
    count = lax.axis_size("dp")
    half_width = model_width // 2
    tensor_part = lax.axis_index("tensor")
    position = lax.axis_index("dp")
    cut = width * EXCHANGED[0] // EXCHANGED[1]

    slots = first_phase(value_weight[:, :cut])
    gathered = lax.all_gather(value_weight[:, cut:], ("dp", "tensor"), axis=0)
    gathered = gathered.reshape(count, 2, value_weight.shape[0], width - cut)

    most = 9 * count // 16
    single_run = count - most == tenant_count - 1
    if value_weight.shape[0] % 64 == 0 and single_run:
        mine, shared, *blocks = prepare(
            tenant_devices, adapter_of, valid_tokens, adapter_down_maps, adapter_up_maps, cotangent, count
        )
        other = swap_cores(mine)
        scaled_t, term_a = back(mine, other, normed)
        rows = send_blocks_low(blocks)
        held, masks, last = middle_phases(row_parts(slots))
        own_blocks = send_blocks_high(rows)
        low_rank, down_keep, term_b, parts = low_rank_of(
            shared, own_blocks, swap_cores(own_blocks), mine, term_a, normed, rank
        )
        got, plan = last_phase(held, masks, last)
        strip = sum_to_strip(row_sums(parts))
        total = gather_strips(fence(strip, gathered)).astype(jnp.float32)
        grad_a = jnp.where(shared[0] > 0, total[:, :half_width], term_a)[None]
        grad_b = jnp.where(shared[0] > 0, total[:, half_width:], term_b)[None]
    else:
        slot_ends = jnp.cumsum(tenant_devices)
        tenant_slot = jnp.sum((slot_ends <= position).astype(jnp.int32))
        picker = (jnp.arange(tenant_count, dtype=jnp.int32) == tenant_slot).astype(jnp.int32)
        first_device = jnp.sum(picker * (slot_ends - tenant_devices))
        adapter_index = jnp.sum(picker * adapter_of)
        valid_count = jnp.sum(picker * valid_tokens)
        offsets = (position - first_device) * row_count + jnp.arange(row_count, dtype=jnp.int32)
        keep_rows = offsets < valid_count
        up_matrix = lax.dynamic_index_in_dim(adapter_up_maps, adapter_index, 0, keepdims=False)
        masked = jnp.where(keep_rows[:, None], cotangent, jnp.zeros_like(cotangent))
        mine = jnp.concatenate([masked, up_matrix])
        other = swap_cores(mine)
        scaled_t, term_a = back(mine, other, normed)
        down_maps = lax.all_gather(adapter_down_maps, "dp", axis=0, tiled=True)
        down_map = lax.dynamic_slice_in_dim(down_maps, adapter_index * rank, rank, 1)
        down_keep = lax.dynamic_slice_in_dim(down_map, tensor_part * half_width, half_width, 0)
        low_rank = dot(normed, down_map, 1, 0).astype(jnp.bfloat16)
        term_b = 2.0 * dot(low_rank, masked, 0, 0)
        marks = picker.astype(jnp.float32)[:, None, None]
        totals = lax.psum((marks * term_a[None], marks * term_b[None]), "dp")
        grad_a = lax.dynamic_index_in_dim(totals[0], tenant_slot, 0, keepdims=True)
        grad_b = lax.dynamic_index_in_dim(totals[1], tenant_slot, 0, keepdims=True)
        held, masks, last = middle_phases(row_parts(slots))
        got, plan = last_phase(held, masks, last)

    own, theirs, weight = forward(held + got, plan, normed, low_rank, mine, 0, cut)
    part = jnp.reshape(tensor_part, (1,))
    values = last_values(part, gathered, normed, low_rank, mine[row_count:], own, swap_cores(theirs))
    gradient = input_gradient(part, weight, gathered, mine, other, scaled_t, down_keep)
    return (values, gradient, grad_a, grad_b)


def solution(mesh):
    return jax.shard_map(
        shards,
        mesh=mesh,
        in_specs=(
            P(("groups", "dp"), None),
            P(("groups", "dp"), "tensor"),
            P("dp", "tensor"),
            P("dp", "groups"),
            P("groups", None, "tensor"),
            P("groups"),
            P("groups"),
            P("groups"),
        ),
        out_specs=(
            P(("groups", "dp"), "tensor"),
            P(("groups", "dp"), "tensor"),
            P(("groups", "dp"), None, "tensor"),
            P(("groups", "dp"), None, "tensor"),
        ),
        check_vma=False,
    )
```
